32 devices in a mesh: grp: 2 (over y), row: 8 (over z, x), col: 1, sub: 2 (over core).
Axes of the slice: x: 2, y: 2, z: 4, core: 2. Of those that a mesh axis runs over, the one named last changes fastest.
Arguments:
- pair: float32 [256, 128, 128], P(('grp', 'row'), 'col'), parts along dimension 0, may hold values from -6 to 6
- mask: int32 [256], P('grp'), parts along dimension 0, may hold values from 0 to 1, as said below
- w_edges: bfloat16 [128, 4, 128], P(None, None, 'sub'), may hold values from -0.5 to 0.5
- w_outgate: bfloat16 [128, 128], replicated, may hold values from -0.5 to 0.5
- w_outproj: bfloat16 [128, 128], replicated, may hold values from -0.5 to 0.5
- w_attend: bfloat16 [128, 4, 128], P(None, None, 'sub'), may hold values from -0.5 to 0.5
- w_bias: bfloat16 [128, 4], P(None, 'sub'), may hold values from -16 to 16
- w_attout: bfloat16 [128, 128], P('sub'), may hold values from -0.5 to 0.5
Outputs:
- updated: float32 [256, 128, 128], P(('grp', 'row'), 'col'), parts along dimension 0
The draws below stay inside these ranges and needn't reach their ends.
There are 2 independent parts, one for each index of `grp`. The reference program is written for one: setup_inputs(seed, part) draws one part's arguments, and reference() takes and returns one part's arrays. A program takes and returns all parts, laid end to end along the dimension named above; an argument that names none is the same for every part. Nothing has to cross between parts.
Inputs may be any that keep to these rules, and one draw needn't show every extreme that they name: mask is 1 for residues 0 to L-1 and 0 after, with L of 64 to 128.
All inputs are finite; a program needn't handle non-finite values.
Results may differ from the reference program's by a relative error of at most 0.025.
Values may be sent and summed in bfloat16 or wider, within the bound.
A program may use at most 64 MiB of HBM per device.

```python
import jax
import jax.numpy as jnp
from jax import lax

C = 128
HID = 128
H = 4
DH = 32
N = 128


def draw_mask(key, part):
    key = jax.random.fold_in(key, 11)
    length = jax.random.randint(key, (), N // 2, N + 1)
    return (jnp.arange(N) < length).astype(jnp.int32)


def draw_w_bias(key, part):
    key = jax.random.fold_in(key, 23)
    values = jax.random.normal(key, (C, H), jnp.float32)
    return jnp.clip(values / jnp.sqrt(jnp.float32(C)), -16.0, 16.0).astype(jnp.bfloat16)


def steps_of(rng, extent, split, smallest, top_value):
    factor_of = 1.0
    for dim, blocks in split:
        steps = jax.random.uniform(jax.random.fold_in(jax.random.fold_in(rng, 6), dim), (blocks,), jnp.float32, smallest / len(split), top_value / len(split))
        factor_of = factor_of * jnp.repeat(jnp.exp(steps), extent[dim] // blocks).reshape((-1,) + (1,) * (len(extent) - 1 - dim))
    return factor_of


def gaussian(stream_key, extent, scale, limit, pieces=(), kind=jnp.bfloat16):
    loudness = steps_of(stream_key, extent, pieces, -0.22, 0.18) if pieces else 1.0
    entries = jax.random.normal(stream_key, extent, jnp.float32) * scale * loudness
    return jnp.minimum(jnp.maximum(entries, -limit), limit).astype(kind)


def setup_inputs(seed: int = 0, part: int = 0) -> dict:
    seeds = jax.random.split(jax.random.key(seed), 9)
    part_keys = jax.random.split(jax.random.fold_in(seeds[8], part), 9)
    return {
        "pair": gaussian(part_keys[0], (N, N, C), 1.0, 6.0, ((0, 8),), jnp.float32),
        "mask": draw_mask(jax.random.fold_in(jax.random.fold_in(seeds[8], part), 71), part),
        "w_edges": gaussian(seeds[2], (C, 4, HID), C ** -0.5, 0.5, ((2, 2),)),
        "w_outgate": gaussian(seeds[3], (C, C), C ** -0.5, 0.5),
        "w_outproj": gaussian(seeds[4], (HID, C), HID ** -0.5, 0.5),
        "w_attend": gaussian(seeds[5], (C, 4, H * DH), C ** -0.5, 0.5, ((2, 2),)),
        "w_bias": draw_w_bias(jax.random.fold_in(seeds[8], 71), part),
        "w_attout": gaussian(seeds[7], (H * DH, C), (H * DH) ** -0.5, 0.5, ((0, 2),)),
    }


EPS = 1e-05

def layer_norm(values, axis):
    mean = lax.optimization_barrier(jnp.mean(values, axis=axis, keepdims=True))
    centred = values - mean
    variance = lax.optimization_barrier(jnp.mean(centred * centred, axis=axis, keepdims=True))
    return centred * lax.rsqrt(variance + EPS)

def project(normed, weight):
    return jnp.dot(normed, weight, preferred_element_type=jnp.float32)

def reference(pair, mask, w_edges, w_outgate, w_outproj, w_attend, w_bias, w_attout):
    mfloat = mask.astype(jnp.float32)
    pmask = (mfloat[:, None] * mfloat[None, :])[:, :, None]
    normed = layer_norm(pair, -1).astype(jnp.bfloat16)
    left = (pmask * jax.nn.sigmoid(project(normed, w_edges[:, 0])) * project(normed, w_edges[:, 1])).astype(jnp.bfloat16)
    right = (pmask * jax.nn.sigmoid(project(normed, w_edges[:, 2])) * project(normed, w_edges[:, 3])).astype(jnp.bfloat16)
    edges = jnp.einsum('ikh,jkh->ijh', left.astype(jnp.float32), right.astype(jnp.float32))
    edgenorm = layer_norm(edges, -1).astype(jnp.bfloat16)
    first = pair + jax.nn.sigmoid(project(normed, w_outgate)) * project(edgenorm, w_outproj)
    second = layer_norm(first, -1).astype(jnp.bfloat16)
    query = project(second, w_attend[:, 0]).astype(jnp.bfloat16)
    keyed = project(second, w_attend[:, 1]).astype(jnp.bfloat16)
    valued = project(second, w_attend[:, 2]).astype(jnp.bfloat16)
    attgate = project(second, w_attend[:, 3])
    bias = project(second, w_bias).astype(jnp.bfloat16)
    bias_heads = jnp.transpose(bias.astype(jnp.float32), (2, 0, 1))
    maskbias = 1000000000.0 * (mfloat - 1.0)
    block = 16

    def attend_block(index):
        start = (index * block).astype(jnp.int32)
        qblock = lax.dynamic_slice_in_dim(query, start, block, 0).reshape(block, N, H, DH).astype(jnp.float32)
        kblock = lax.dynamic_slice_in_dim(keyed, start, block, 0).reshape(block, N, H, DH).astype(jnp.float32)
        vblock = lax.dynamic_slice_in_dim(valued, start, block, 0).reshape(block, N, H, DH).astype(jnp.float32)
        scores = jnp.einsum('ijhd,ikhd->ihjk', qblock, kblock) / jnp.sqrt(jnp.float32(DH))
        scores = scores + bias_heads[None] + maskbias[None, None, None, :]
        weights = jax.nn.softmax(scores, axis=-1).astype(jnp.bfloat16)
        output = jnp.einsum('ihjk,ikhd->ijhd', weights.astype(jnp.float32), vblock)
        return output.reshape(block, N, H * DH)
    attended = lax.map(attend_block, jnp.arange(N // block, dtype=jnp.int32)).reshape(N, N, H * DH)
    mixed = (attended * jax.nn.sigmoid(attgate)).astype(jnp.bfloat16)
    return first + project(mixed, w_attout)
```

```python
import jax
import jax.numpy as jnp
from jax import lax
from jax.experimental import pallas as pl
from jax.experimental.pallas import tpu as pltpu
from jax.sharding import PartitionSpec as P

EPS = 1e-05
MESH = pl.DeviceIdType.MESH
CHUNKS = 4


def dot(a, b):
    return jnp.dot(a, b, preferred_element_type=jnp.float32)


def norm_rows(values):
    mean = jnp.mean(values, axis=0, keepdims=True)
    centred = values - mean
    variance = jnp.mean(centred * centred, axis=0, keepdims=True)
    return centred * lax.rsqrt(variance + EPS)


def turned(ref_value):
    return ref_value.astype(jnp.float32).T


def fused_kernel(
    pair_ref, mask_ref, smask_ref, we_ref, wog_ref, wop_ref, wa_ref, wb_ref, wo_ref,
    out_ref,
    wet, wa_all, wb_all, wo_all, sent, got, wide, pair_t, normed_t, gates, back, owned, wide2,
    first_t, second_t, bias_rows, bias_send, bias_got, bias_t, query_t, keyed, value_t, attgate_t,
    w_send, w_recv, a_send, a_recv, b_send, b_recv, c_send, c_recv, o_send, o_recv,
):
    row = lax.axis_index("row")
    sub = lax.axis_index("sub")
    other = 1 - sub
    count = 8
    rows = 16
    half = 8
    step = rows // CHUNKS

    def at_row(offset):
        return lax.rem(row + offset, count)

    def from_row(offset):
        return lax.rem(row + count - offset, count)

    barrier = pltpu.get_barrier_semaphore()
    peers = [(o, d) for o in range(count) for d in range(2) if (o, d) != (0, 0)]

    def peer_sub(d):
        return sub if d == 0 else other

    for o, d in peers:
        pl.semaphore_signal(
            barrier, inc=1, device_id={"row": at_row(o), "sub": peer_sub(d)}, device_id_type=MESH
        )

    turned_we = turned(we_ref[...])
    gate_rows = [turned_we[128 * lr + 8 * p:128 * lr + 8 * p + 8] for p in range(8) for lr in range(2)]
    value_rows = [
        turned_we[128 * lr + 64 + 8 * p:128 * lr + 64 + 8 * p + 8] for p in range(8) for lr in range(2)
    ]
    wet[...] = jnp.concatenate(gate_rows + value_rows, axis=0).astype(jnp.bfloat16)
    mask_lanes = mask_ref[...].astype(jnp.float32)

    def edge_row(i, carry):
        x = pair_ref[i].T
        pair_t[i] = x
        normed = norm_rows(x).astype(jnp.bfloat16)
        normed_t[i] = normed
        projected = dot(wet[...], normed)
        mask_row = smask_ref[row * rows + i].astype(jnp.float32)
        edge = (mask_lanes * mask_row) * jax.nn.sigmoid(projected[:128]) * projected[128:]
        edge = edge.astype(jnp.bfloat16)
        for p in range(8):
            sent[p, i] = edge[16 * p:16 * p + 16]
        return carry

    def a_copy(o, c, slot_from, slot_to):
        part = pl.ds(c * step, step)
        return pltpu.make_async_remote_copy(
            src_ref=sent.at[slot_from, part],
            dst_ref=got.at[slot_to, part],
            send_sem=a_send.at[o, c],
            recv_sem=a_recv.at[o, c],
            device_id={"row": at_row(o)},
            device_id_type=MESH,
        )

    def w_copy(k, src, dst):
        return pltpu.make_async_remote_copy(
            src_ref=src, dst_ref=dst, send_sem=w_send.at[k], recv_sem=w_recv.at[k],
            device_id={"sub": other}, device_id_type=MESH,
        )

    order = [4, 3, 5, 2, 6, 1, 7]
    for c in range(CHUNKS):
        lax.fori_loop(c * step, (c + 1) * step, edge_row, 0, unroll=2)
        if c == 0:
            pl.semaphore_wait(barrier, len(peers))
        for o in order:
            a_copy(o, c, at_row(o), row).start()
    for k, (src, dst) in enumerate(((wa_ref, wa_all), (wb_ref, wb_all), (wo_ref, wo_all))):
        w_copy(k, src, dst.at[sub]).start()

    wa_all[sub] = wa_ref[...]
    wb_all[sub] = wb_ref[...]
    wo_all[sub] = wo_ref[...]
    outgate_t = turned(wog_ref[...]).astype(jnp.bfloat16)

    def gate_row(i, carry):
        gates[i] = jax.nn.sigmoid(dot(outgate_t, normed_t[sub * half + i]))
        return carry

    lax.fori_loop(0, half, gate_row, 0, unroll=2)
    outproj_t = turned(wop_ref[...]).astype(jnp.bfloat16)

    wide[pl.ds(pl.multiple_of(row * 256, 256), 256), :] = (
        sent[row].reshape(256, 128).astype(jnp.float32)
    )
    for o in order[::-1]:
        source = from_row(o)
        for c in range(CHUNKS):
            a_copy(o, c, source, source).wait_recv()
        wide[pl.ds(pl.multiple_of(source * 256, 256), 256), :] = (
            got[source].reshape(256, 128).astype(jnp.float32)
        )

    for pair_of in range(4):
        sums = []
        for h in (2 * pair_of, 2 * pair_of + 1):
            left = wide[pl.ds(h, 128, stride=16), :].astype(jnp.bfloat16)
            right = wide[pl.ds(8 + h, 128, stride=16), :].astype(jnp.bfloat16)
            total = lax.dot_general(
                left, right, (((1,), (1,)), ((), ())), preferred_element_type=jnp.float32
            )
            sums.append(total.reshape(16, 8, 128))
        back[:, pl.ds(16 * pair_of, 16), :] = jnp.concatenate(sums, axis=1).astype(jnp.bfloat16)

    def b_copy(k, o, d, src, dst):
        return pltpu.make_async_remote_copy(
            src_ref=back.at[src], dst_ref=owned.at[dst], send_sem=b_send.at[k], recv_sem=b_recv.at[k],
            device_id={"row": at_row(o), "sub": peer_sub(d)}, device_id_type=MESH,
        )

    ranked = [(o, d) for o in order for d in (1, 0)] + [(0, 1)]
    for k, (o, d) in enumerate(ranked):
        b_copy(k, o, d, at_row(o) * 2 + peer_sub(d), sub * 8 + row).start()
    wide2[pl.ds(pl.multiple_of((sub * 8 + row) * 64, 64), 64), :] = (
        back[row * 2 + sub].astype(jnp.float32)
    )

    for k, (src, dst) in enumerate(((wa_ref, wa_all), (wb_ref, wb_all), (wo_ref, wo_all))):
        w_copy(k, src, dst.at[other]).wait_recv()
    wat = [turned(wa_all[s]).astype(jnp.bfloat16) for s in range(2)]
    attend_t = jnp.concatenate(
        [wat[s][64 * q:64 * q + 64] for q in range(4) for s in range(2)], axis=0
    )
    bias_w = wb_all[...].reshape(32, 128)
    attout_t = turned(wo_all[...].reshape(128, 128)).astype(jnp.bfloat16)

    for k in reversed(range(len(ranked))):
        o, d = ranked[k]
        source = peer_sub(d) * 8 + from_row(o)
        b_copy(k, o, d, 0, source).wait_recv()
        wide2[pl.ds(pl.multiple_of(source * 64, 64), 64), :] = owned[source].astype(jnp.float32)

    for i in range(half):
        edgenorm = norm_rows(wide2[pl.ds(i, 128, stride=8), :]).astype(jnp.bfloat16)
        first = pair_t[sub * half + i] + gates[i] * dot(outproj_t, edgenorm)
        first_t[i] = first
        second = norm_rows(first).astype(jnp.bfloat16)
        second_t[i] = second
        bias = dot(bias_w, second)
        for n in range(4):
            r = 16 * (n // 2) + n % 2
            bias_rows[n * 8 + i:n * 8 + i + 1, :] = bias[r:r + 1]
    bias_send[...] = bias_rows[...].astype(jnp.bfloat16)

    def c_copy(k, o, d, dst):
        return pltpu.make_async_remote_copy(
            src_ref=bias_send, dst_ref=bias_got.at[dst], send_sem=c_send.at[k], recv_sem=c_recv.at[k],
            device_id={"row": at_row(o), "sub": peer_sub(d)}, device_id_type=MESH,
        )

    for k, (o, d) in enumerate(ranked):
        c_copy(k, o, d, row * 2 + sub).start()

    def project_row(i, carry):
        projected = dot(attend_t, second_t[i])
        query_t[i] = projected[:128].astype(jnp.bfloat16)
        keyed[i] = projected[128:256].T.astype(jnp.bfloat16)
        value_t[i] = projected[256:384].astype(jnp.bfloat16)
        attgate_t[i] = jax.nn.sigmoid(projected[384:])
        return carry

    lax.fori_loop(0, half, project_row, 0, unroll=2)

    mine = row * 2 + sub
    bias_got[mine] = bias_send[...]
    for k in reversed(range(len(ranked))):
        o, d = ranked[k]
        c_copy(k, o, d, from_row(o) * 2 + peer_sub(d)).wait_recv()
    maskbias = 1000000000.0 * (mask_lanes - 1.0)
    all_bias = bias_got[...].astype(jnp.float32)
    for n in range(4):
        bias_t[n] = (all_bias[:, n * 8:n * 8 + 8, :].reshape(128, 128) + maskbias).T

    scale = 1.0 / (32.0 ** 0.5)

    def o_copy(i, at):
        return pltpu.make_async_remote_copy(
            src_ref=out_ref.at[at * half + i], dst_ref=out_ref.at[at * half + i],
            send_sem=o_send.at[i], recv_sem=o_recv.at[i],
            device_id={"sub": other}, device_id_type=MESH,
        )

    def attend_row(i, carry):
        query = query_t[i]
        key = keyed[i]
        value = value_t[i]
        nothing = jnp.zeros((32, 128), jnp.bfloat16)
        mixed = []
        for n in range(4):
            head = jnp.concatenate(
                [query[32 * m:32 * m + 32] if m == n else nothing for m in range(4)], axis=0
            )
            scores = dot(key, head) * scale + bias_t[n]
            top = jnp.max(scores, axis=0, keepdims=True)
            weights = jnp.exp(scores - top)
            total = jnp.sum(weights, axis=0, keepdims=True)
            mixed.append(dot(value[32 * n:32 * n + 32], weights.astype(jnp.bfloat16)) / total)
        mixed = (jnp.concatenate(mixed, axis=0) * attgate_t[i]).astype(jnp.bfloat16)
        out_ref[sub * half + i] = (first_t[i] + dot(attout_t, mixed)).T
        o_copy(i, sub).start()
        return carry

    lax.fori_loop(0, half, attend_row, 0, unroll=2)

    for k, (src, dst) in enumerate(((wa_ref, wa_all), (wb_ref, wb_all), (wo_ref, wo_all))):
        w_copy(k, src, dst.at[sub]).wait_send()
    for c in range(CHUNKS):
        for o in order:
            a_copy(o, c, at_row(o), row).wait_send()
    for k, (o, d) in enumerate(ranked):
        b_copy(k, o, d, at_row(o) * 2 + peer_sub(d), sub * 8 + row).wait_send()
        c_copy(k, o, d, row * 2 + sub).wait_send()
    for i in range(half):
        o_copy(i, sub).wait_send()
        o_copy(i, other).wait_recv()


def fused_body(pair, mask, w_edges, w_outgate, w_outproj, w_attend, w_bias, w_attout):
    f32, bf16 = jnp.float32, jnp.bfloat16
    vmem = pl.BlockSpec(memory_space=pltpu.VMEM)
    bias_rows = jnp.pad(w_bias.T, ((0, 14), (0, 0)))
    dma = pltpu.SemaphoreType.DMA
    return pl.pallas_call(
        fused_kernel,
        out_shape=jax.ShapeDtypeStruct(pair.shape, f32),
        in_specs=[vmem, vmem, pl.BlockSpec(memory_space=pltpu.SMEM)] + [vmem] * 6,
        out_specs=vmem,
        scratch_shapes=[
            pltpu.VMEM((256, 128), bf16),
            pltpu.VMEM((2, 128, 256), bf16),
            pltpu.VMEM((2, 16, 128), bf16),
            pltpu.VMEM((2, 64, 128), bf16),
            pltpu.VMEM((8, 16, 16, 128), bf16),
            pltpu.VMEM((8, 16, 16, 128), bf16),
            pltpu.VMEM((2048, 128), f32),
            pltpu.VMEM((16, 128, 128), f32),
            pltpu.VMEM((16, 128, 128), bf16),
            pltpu.VMEM((8, 128, 128), f32),
            pltpu.VMEM((16, 64, 128), bf16),
            pltpu.VMEM((16, 64, 128), bf16),
            pltpu.VMEM((1024, 128), f32),
            pltpu.VMEM((8, 128, 128), f32),
            pltpu.VMEM((8, 128, 128), bf16),
            pltpu.VMEM((32, 128), f32),
            pltpu.VMEM((32, 128), bf16),
            pltpu.VMEM((16, 32, 128), bf16),
            pltpu.VMEM((4, 128, 128), f32),
            pltpu.VMEM((8, 128, 128), bf16),
            pltpu.VMEM((8, 128, 128), bf16),
            pltpu.VMEM((8, 128, 128), bf16),
            pltpu.VMEM((8, 128, 128), f32),
            dma((3,)), dma((3,)),
            dma((8, CHUNKS)), dma((8, CHUNKS)),
            dma((15,)), dma((15,)),
            dma((15,)), dma((15,)),
            dma((8,)), dma((8,)),
        ],
        compiler_params=pltpu.CompilerParams(
            collective_id=0, has_side_effects=True, vmem_limit_bytes=40 * 1024 * 1024
        ),
        name="window",
    )(
        pair, mask.reshape(1, 128), mask, w_edges.reshape(128, 256), w_outgate, w_outproj,
        w_attend.reshape(128, 256), bias_rows, w_attout,
    )


def fits(mesh):
    sizes = dict(mesh.shape)
    return sizes["col"] == 1 and sizes["row"] == 8 and sizes["sub"] == 2


def layer_norm(values, axis):
    mean = jnp.mean(values, axis=axis, keepdims=True)
    centred = values - mean
    variance = jnp.mean(centred * centred, axis=axis, keepdims=True)
    return centred * lax.rsqrt(variance + EPS)


def body(pair, mask, w_edges, w_outgate, w_outproj, w_attend, w_bias, w_attout):
    rows, cols, channels = pair.shape
    row_start = lax.axis_index("row") * rows
    col_start = lax.axis_index("col") * cols
    mfloat = mask.astype(jnp.float32)
    mask_rows = lax.dynamic_slice_in_dim(mfloat, row_start, rows, 0)
    mask_cols = lax.dynamic_slice_in_dim(mfloat, col_start, cols, 0)
    pmask = mask_rows[:, None] * mask_cols[None, :]
    normed = layer_norm(pair, -1).astype(jnp.bfloat16)
    projected = jnp.einsum("ijc,cqh->qhij", normed, w_edges, preferred_element_type=jnp.float32)
    left = (pmask * jax.nn.sigmoid(projected[0]) * projected[1]).astype(jnp.bfloat16)
    right = (pmask * jax.nn.sigmoid(projected[2]) * projected[3]).astype(jnp.bfloat16)
    row_count = lax.axis_size("row")
    col_count = lax.axis_size("col")
    devices = row_count * col_count
    hidden = left.shape[0]
    if devices % hidden == 0:
        groups = 1
        copies = devices // hidden
    else:
        groups = hidden // devices
        copies = 1
    share = rows // copies
    left_send = left.reshape(devices, groups * share, cols)
    right_send = jnp.repeat(right, copies, axis=0).reshape(devices, groups, rows, cols)
    left_got, right_got = (
        lax.all_to_all(left_send, ("row", "col"), split_axis=0, concat_axis=0, tiled=True),
        lax.all_to_all(right_send, ("row", "col"), split_axis=0, concat_axis=0, tiled=True),
    )
    left_owned = left_got.reshape(row_count, col_count, groups, share, cols)
    left_owned = left_owned.transpose(2, 0, 3, 1, 4).reshape(
        groups, row_count * share, col_count * cols
    )
    right_owned = right_got.reshape(row_count, col_count, groups, rows, cols)
    right_owned = right_owned.transpose(2, 0, 3, 1, 4).reshape(
        groups, row_count * rows, col_count * cols
    )
    owned_sums = jnp.einsum(
        "gak,gjk->gaj", left_owned, right_owned, preferred_element_type=jnp.float32
    )
    outgoing = owned_sums.reshape(groups, row_count, share, col_count, cols)
    outgoing = outgoing.transpose(1, 3, 0, 2, 4).reshape(devices, groups * share, cols)
    returned = lax.all_to_all(outgoing, ("row", "col"), split_axis=0, concat_axis=0, tiled=True)
    edges = returned.reshape(hidden, rows, cols)
    all_edges = lax.all_gather(edges, "sub", axis=0, tiled=True)
    edgenorm = layer_norm(all_edges, 0).astype(jnp.bfloat16)
    outgate = jax.nn.sigmoid(
        jnp.einsum("ijc,cd->ijd", normed, w_outgate, preferred_element_type=jnp.float32)
    )
    first = pair + outgate * jnp.einsum(
        "hij,hd->ijd", edgenorm, w_outproj, preferred_element_type=jnp.float32
    )
    second = layer_norm(first, -1).astype(jnp.bfloat16)
    attproj = jnp.einsum("ijc,cqe->qije", second, w_attend, preferred_element_type=jnp.float32)
    query = attproj[0].astype(jnp.bfloat16)
    keyed = attproj[1].astype(jnp.bfloat16)
    valued = attproj[2].astype(jnp.bfloat16)
    attgate = attproj[3]
    bias = jnp.einsum("ijc,ch->hij", second, w_bias, preferred_element_type=jnp.float32).astype(
        jnp.bfloat16
    )
    all_keys, all_values = (
        lax.all_gather(keyed, "col", axis=1, tiled=True),
        lax.all_gather(valued, "col", axis=1, tiled=True),
    )
    bias_full = lax.all_gather(bias, "col", axis=2, tiled=True)
    bias_every = lax.all_gather(bias_full, "row", axis=1, tiled=True)
    bias_strip = lax.dynamic_slice_in_dim(bias_every, col_start, cols, 1)
    heads = w_bias.shape[1]
    width = query.shape[2]
    head_size = width // heads
    total = all_keys.shape[1]
    query_heads = query.reshape(rows, cols, heads, head_size)
    key_heads = all_keys.reshape(rows, total, heads, head_size)
    value_heads = all_values.reshape(rows, total, heads, head_size)
    maskbias = 1000000000.0 * (mfloat - 1.0)
    scores = jnp.einsum(
        "ijhd,ikhd->hijk", query_heads, key_heads, preferred_element_type=jnp.float32
    )
    scores = scores / jnp.sqrt(jnp.float32(head_size))
    scores = scores + bias_strip.astype(jnp.float32)[:, None, :, :] + maskbias[None, None, None, :]
    weights = jax.nn.softmax(scores, axis=-1).astype(jnp.bfloat16)
    attended = jnp.einsum(
        "hijk,ikhd->ijhd", weights, value_heads, preferred_element_type=jnp.float32
    )
    mixed = (attended.reshape(rows, cols, width) * jax.nn.sigmoid(attgate)).astype(jnp.bfloat16)
    terms = jnp.einsum("ije,ec->ijc", mixed, w_attout, preferred_element_type=jnp.float32)
    summed = lax.psum(terms.astype(jnp.bfloat16), "sub").astype(jnp.float32)
    return first + summed


def solution(mesh):
    placed = (
        P(("grp", "row"), "col", None),
        P("grp"),
        P(None, None, "sub"),
        P(),
        P(),
        P(None, None, "sub"),
        P(None, "sub"),
        P("sub", None),
    )
    whole = jax.shard_map(
        body, mesh=mesh, in_specs=placed, out_specs=P(("grp", "row"), "col", None), check_vma=False
    )
    if not fits(mesh):
        return whole
    fused = jax.shard_map(
        fused_body, mesh=mesh, in_specs=placed, out_specs=P(("grp", "row"), "col", None), check_vma=False
    )
    parts = mesh.shape["grp"]
    shapes = [
        (128 * parts, 128, 128), (128 * parts,), (128, 4, 128), (128, 128), (128, 128), (128, 4, 128),
        (128, 4), (128, 128),
    ]

    def run(*arrays):
        same = [a.shape for a in arrays] == shapes
        return (fused if same else whole)(*arrays)

    return run
```

```python
import jax
import jax.numpy as jnp
from jax import lax
from jax.experimental import pallas as pl
from jax.experimental.pallas import tpu as pltpu
from jax.sharding import PartitionSpec as P

EPS = 1e-05
MESH = pl.DeviceIdType.MESH
CHUNKS = 4


def dot(a, b):
    return jnp.dot(a, b, preferred_element_type=jnp.float32)


def norm_rows(values):
    mean = jnp.mean(values, axis=0, keepdims=True)
    centred = values - mean
    variance = jnp.mean(centred * centred, axis=0, keepdims=True)
    return centred * lax.rsqrt(variance + EPS)


def turned(ref_value):
    return ref_value.astype(jnp.float32).T


def fused_kernel(
    pair_hbm, mask_ref, smask_ref, we_ref, wog_ref, wop_ref, wa_ref, wb_ref, wo_ref,
    out_ref,
    pair_v, wa_all, wb_all, wo_all, sent_l, sent_r, got_l, got_r, wide_l, wide_r, pair_t, normed_t,
    gates, back, owned, wide2,
    first_t, second_t, bias_rows, bias_send, bias_got, bias_t, query_t, keyed, value_t, attgate_t,
    p_sem, w_send, w_recv, l_send, l_recv, r_send, r_recv, b_send, b_recv, c_send, c_recv,
    o_send, o_recv,
):
    row = lax.axis_index("row")
    sub = lax.axis_index("sub")
    other = 1 - sub
    side = lax.div(row, 4)
    place = lax.rem(row, 4)
    rows = 16
    half = 8
    step = rows // CHUNKS

    def p_copy(c):
        part = pl.ds(c * step, step)
        return pltpu.make_async_copy(pair_hbm.at[part], pair_v.at[part], p_sem.at[c])

    for c in range(CHUNKS):
        p_copy(c).start()

    def place_to(dg):
        return lax.rem(place + dg, 4)

    def place_from(dg):
        return lax.rem(place + 4 - dg, 4)

    def side_of(ds):
        return side if ds == 0 else 1 - side

    def row_to(ds, dg):
        return side_of(ds) * 4 + place_to(dg)

    def row_from(ds, dg):
        return side_of(ds) * 4 + place_from(dg)

    def peer_sub(d):
        return sub if d == 0 else other

    far = [(1, 3), (1, 2), (1, 1), (1, 0)]
    near = [(0, 3), (0, 2), (0, 1)]
    every = [(ds, dg, d) for ds, dg in far + near for d in (1, 0)] + [(0, 0, 1)]
    around = [(dg, d) for dg in (3, 2, 1) for d in (1, 0)] + [(0, 1)]

    barrier = pltpu.get_barrier_semaphore()
    for ds, dg, d in every:
        pl.semaphore_signal(
            barrier, inc=1, device_id={"row": row_to(ds, dg), "sub": peer_sub(d)}, device_id_type=MESH
        )

    mask_lanes = mask_ref[...].astype(jnp.float32)
    edge_w = we_ref[...]

    def edge_row(i):
        x = pair_v[i].T
        pair_t[i] = x
        normed = norm_rows(x).astype(jnp.bfloat16)
        normed_t[i] = normed
        projected = dot(edge_w, normed)
        mask_row = mask_lanes * smask_ref[row * rows + i].astype(jnp.float32)
        for q, sent in ((0, sent_l), (128, sent_r)):
            edge = mask_row * jax.nn.sigmoid(projected[q:q + 64]) * projected[q + 64:q + 128]
            edge = edge.astype(jnp.bfloat16)
            for g in range(4):
                sent[g, i] = edge[16 * g:16 * g + 16]

    def r_copy(ds, dg, c, slot_from, slot_to):
        part = pl.ds(c * step, step)
        return pltpu.make_async_remote_copy(
            src_ref=sent_r.at[slot_from, part], dst_ref=got_r.at[slot_to, part],
            send_sem=r_send.at[ds * 4 + dg, c], recv_sem=r_recv.at[ds * 4 + dg, c],
            device_id={"row": row_to(ds, dg)}, device_id_type=MESH,
        )

    def l_copy(dg, c, slot_from, slot_to):
        part = pl.ds(c * step, step)
        return pltpu.make_async_remote_copy(
            src_ref=sent_l.at[slot_from, part], dst_ref=got_l.at[slot_to, part],
            send_sem=l_send.at[dg, c], recv_sem=l_recv.at[dg, c],
            device_id={"row": row_to(0, dg)}, device_id_type=MESH,
        )

    def w_copy(k, at):
        src, dst = ((wa_ref, wa_all), (wb_ref, wb_all), (wo_ref, wo_all))[k]
        return pltpu.make_async_remote_copy(
            src_ref=src, dst_ref=dst.at[at], send_sem=w_send.at[k], recv_sem=w_recv.at[k],
            device_id={"sub": other}, device_id_type=MESH,
        )

    for c in range(CHUNKS):
        p_copy(c).wait()
        for i in range(c * step, (c + 1) * step):
            edge_row(i)
        if c == 0:
            pl.semaphore_wait(barrier, len(every))
        for ds, dg in far + near:
            r_copy(ds, dg, c, place_to(dg), row).start()
            if ds == 0:
                l_copy(dg, c, place_to(dg), place).start()
    for k in range(3):
        w_copy(k, sub).start()

    wa_all[sub] = wa_ref[...]
    wb_all[sub] = wb_ref[...]
    wo_all[sub] = wo_ref[...]
    outgate_t = turned(wog_ref[...]).astype(jnp.bfloat16)
    for i in range(half):
        gates[i] = jax.nn.sigmoid(dot(outgate_t, normed_t[sub * half + i]))
    outproj_t = turned(wop_ref[...]).astype(jnp.bfloat16)

    def widen(dst, at, block):
        dst[pl.ds(pl.multiple_of(at * 256, 256), 256), :] = (
            block.reshape(256, 128).astype(jnp.float32)
        )

    widen(wide_l, place, sent_l[place])
    widen(wide_r, row, sent_r[place])
    for ds, dg in near[::-1] + far[::-1]:
        source = row_from(ds, dg)
        for c in range(CHUNKS):
            r_copy(ds, dg, c, place_to(dg), source).wait_recv()
        widen(wide_r, source, got_r[source])
        if ds == 0:
            for c in range(CHUNKS):
                l_copy(dg, c, place_to(dg), place_from(dg)).wait_recv()
            widen(wide_l, place_from(dg), got_l[place_from(dg)])

    for pair_of in range(8):
        sums = []
        for h in (2 * pair_of, 2 * pair_of + 1):
            left = wide_l[pl.ds(h, 64, stride=16), :].astype(jnp.bfloat16)
            right = wide_r[pl.ds(h, 128, stride=16), :].astype(jnp.bfloat16)
            total = lax.dot_general(
                left, right, (((1,), (1,)), ((), ())), preferred_element_type=jnp.float32
            )
            sums.append(total.reshape(8, 8, 128))
        back[:, pl.ds(16 * pair_of, 16), :] = jnp.concatenate(sums, axis=1).astype(jnp.bfloat16)

    def b_copy(k, dg, d, src, dst):
        return pltpu.make_async_remote_copy(
            src_ref=back.at[src], dst_ref=owned.at[dst], send_sem=b_send.at[k], recv_sem=b_recv.at[k],
            device_id={"row": row_to(0, dg), "sub": peer_sub(d)}, device_id_type=MESH,
        )

    def widen2(at, block):
        wide2[pl.ds(pl.multiple_of(at * 128, 128), 128), :] = block.astype(jnp.float32)

    for k, (dg, d) in enumerate(around):
        b_copy(k, dg, d, place_to(dg) * 2 + peer_sub(d), sub * 4 + place).start()
    widen2(sub * 4 + place, back[place * 2 + sub])

    for k in range(3):
        w_copy(k, other).wait_recv()
    attend_t = jnp.concatenate(
        [wa_all[s, 64 * q:64 * q + 64] for q in range(4) for s in range(2)], axis=0
    )
    bias_w = wb_all[...].reshape(32, 128)
    attout_t = turned(wo_all[...].reshape(128, 128)).astype(jnp.bfloat16)

    for k in reversed(range(len(around))):
        dg, d = around[k]
        source = peer_sub(d) * 4 + place_from(dg)
        b_copy(k, dg, d, 0, source).wait_recv()
        widen2(source, owned[source])

    for i in range(half):
        edgenorm = norm_rows(wide2[pl.ds(i, 128, stride=8), :]).astype(jnp.bfloat16)
        first = pair_t[sub * half + i] + gates[i] * dot(outproj_t, edgenorm)
        first_t[i] = first
        second = norm_rows(first).astype(jnp.bfloat16)
        second_t[i] = second
        bias = dot(bias_w, second)
        for n in range(4):
            r = 16 * (n // 2) + n % 2
            bias_rows[n * 8 + i:n * 8 + i + 1, :] = bias[r:r + 1]
    bias_send[...] = bias_rows[...].astype(jnp.bfloat16)

    def c_copy(k, at):
        ds, dg, d = every[k]
        return pltpu.make_async_remote_copy(
            src_ref=bias_send, dst_ref=bias_got.at[at], send_sem=c_send.at[k], recv_sem=c_recv.at[k],
            device_id={"row": row_to(ds, dg), "sub": peer_sub(d)}, device_id_type=MESH,
        )

    mine = row * 2 + sub
    for k in range(len(every)):
        c_copy(k, mine).start()
    bias_got[mine] = bias_send[...]

    for i in range(half):
        projected = dot(attend_t, second_t[i])
        query_t[i] = projected[:128].astype(jnp.bfloat16)
        keyed[i] = projected[128:256].T.astype(jnp.bfloat16)
        value_t[i] = projected[256:384].astype(jnp.bfloat16)
        attgate_t[i] = jax.nn.sigmoid(projected[384:])

    for k in reversed(range(len(every))):
        ds, dg, d = every[k]
        c_copy(k, row_from(ds, dg) * 2 + peer_sub(d)).wait_recv()
    maskbias = 1000000000.0 * (mask_lanes - 1.0)
    all_bias = bias_got[...].astype(jnp.float32)
    for n in range(4):
        bias_t[n] = (all_bias[:, n * 8:n * 8 + 8, :].reshape(128, 128) + maskbias).T

    scale = 1.0 / (32.0 ** 0.5)

    def o_copy(i, at):
        return pltpu.make_async_remote_copy(
            src_ref=out_ref.at[at * half + i], dst_ref=out_ref.at[at * half + i],
            send_sem=o_send.at[i], recv_sem=o_recv.at[i],
            device_id={"sub": other}, device_id_type=MESH,
        )

    nothing = jnp.zeros((32, 128), jnp.bfloat16)

    def attend_row(i):
        query = query_t[i]
        key = keyed[i]
        value = value_t[i]
        mixed = []
        for n in range(4):
            head = jnp.concatenate(
                [query[32 * m:32 * m + 32] if m == n else nothing for m in range(4)], axis=0
            )
            scores = dot(key, head) * scale + bias_t[n]
            top = jnp.max(scores, axis=0, keepdims=True)
            weights = jnp.exp(scores - top)
            total = jnp.sum(weights, axis=0, keepdims=True)
            mixed.append(dot(value[32 * n:32 * n + 32], weights.astype(jnp.bfloat16)) / total)
        mixed = (jnp.concatenate(mixed, axis=0) * attgate_t[i]).astype(jnp.bfloat16)
        out_ref[sub * half + i] = (first_t[i] + dot(attout_t, mixed)).T

    for i in range(half):
        attend_row(i)
        if i % 2 == 1:
            o_copy(i - 1, sub).start()
            o_copy(i, sub).start()

    for k in range(3):
        w_copy(k, sub).wait_send()
    for c in range(CHUNKS):
        for ds, dg in far + near:
            r_copy(ds, dg, c, place_to(dg), row).wait_send()
            if ds == 0:
                l_copy(dg, c, place_to(dg), place).wait_send()
    for k, (dg, d) in enumerate(around):
        b_copy(k, dg, d, place_to(dg) * 2 + peer_sub(d), sub * 4 + place).wait_send()
    for k in range(len(every)):
        c_copy(k, mine).wait_send()
    for i in range(half):
        o_copy(i, sub).wait_send()
        o_copy(i, other).wait_recv()


def fused_body(pair, mask, w_edges, w_outgate, w_outproj, w_attend, w_bias, w_attout):
    f32, bf16 = jnp.float32, jnp.bfloat16
    vmem = pl.BlockSpec(memory_space=pltpu.VMEM)
    bias_rows = jnp.pad(w_bias.T, ((0, 14), (0, 0)))
    dma = pltpu.SemaphoreType.DMA
    return pl.pallas_call(
        fused_kernel,
        out_shape=jax.ShapeDtypeStruct(pair.shape, f32),
        in_specs=[pl.BlockSpec(memory_space=pltpu.HBM), vmem, pl.BlockSpec(memory_space=pltpu.SMEM)]
        + [vmem] * 6,
        out_specs=vmem,
        scratch_shapes=[
            pltpu.VMEM((16, 128, 128), f32),
            pltpu.VMEM((2, 256, 128), bf16),
            pltpu.VMEM((2, 16, 128), bf16),
            pltpu.VMEM((2, 64, 128), bf16),
            pltpu.VMEM((4, 16, 16, 128), bf16),
            pltpu.VMEM((4, 16, 16, 128), bf16),
            pltpu.VMEM((4, 16, 16, 128), bf16),
            pltpu.VMEM((8, 16, 16, 128), bf16),
            pltpu.VMEM((1024, 128), f32),
            pltpu.VMEM((2048, 128), f32),
            pltpu.VMEM((16, 128, 128), f32),
            pltpu.VMEM((16, 128, 128), bf16),
            pltpu.VMEM((8, 128, 128), f32),
            pltpu.VMEM((8, 128, 128), bf16),
            pltpu.VMEM((8, 128, 128), bf16),
            pltpu.VMEM((1024, 128), f32),
            pltpu.VMEM((8, 128, 128), f32),
            pltpu.VMEM((8, 128, 128), bf16),
            pltpu.VMEM((32, 128), f32),
            pltpu.VMEM((32, 128), bf16),
            pltpu.VMEM((16, 32, 128), bf16),
            pltpu.VMEM((4, 128, 128), f32),
            pltpu.VMEM((8, 128, 128), bf16),
            pltpu.VMEM((8, 128, 128), bf16),
            pltpu.VMEM((8, 128, 128), bf16),
            pltpu.VMEM((8, 128, 128), f32),
            dma((CHUNKS,)),
            dma((3,)), dma((3,)),
            dma((4, CHUNKS)), dma((4, CHUNKS)),
            dma((8, CHUNKS)), dma((8, CHUNKS)),
            dma((7,)), dma((7,)),
            dma((15,)), dma((15,)),
            dma((8,)), dma((8,)),
        ],
        compiler_params=pltpu.CompilerParams(
            collective_id=0, has_side_effects=True, vmem_limit_bytes=40 * 1024 * 1024
        ),
        name="window",
    )(
        pair, mask.reshape(1, 128), mask, w_edges.transpose(1, 2, 0).reshape(256, 128), w_outgate,
        w_outproj, w_attend.transpose(1, 2, 0).reshape(256, 128), bias_rows, w_attout,
    )


def fits(mesh):
    sizes = dict(mesh.shape)
    return sizes["col"] == 1 and sizes["row"] == 8 and sizes["sub"] == 2


def layer_norm(values, axis):
    mean = jnp.mean(values, axis=axis, keepdims=True)
    centred = values - mean
    variance = jnp.mean(centred * centred, axis=axis, keepdims=True)
    return centred * lax.rsqrt(variance + EPS)


def body(pair, mask, w_edges, w_outgate, w_outproj, w_attend, w_bias, w_attout):
    rows, cols, channels = pair.shape
    row_start = lax.axis_index("row") * rows
    col_start = lax.axis_index("col") * cols
    mfloat = mask.astype(jnp.float32)
    mask_rows = lax.dynamic_slice_in_dim(mfloat, row_start, rows, 0)
    mask_cols = lax.dynamic_slice_in_dim(mfloat, col_start, cols, 0)
    pmask = mask_rows[:, None] * mask_cols[None, :]
    normed = layer_norm(pair, -1).astype(jnp.bfloat16)
    projected = jnp.einsum("ijc,cqh->qhij", normed, w_edges, preferred_element_type=jnp.float32)
    left = (pmask * jax.nn.sigmoid(projected[0]) * projected[1]).astype(jnp.bfloat16)
    right = (pmask * jax.nn.sigmoid(projected[2]) * projected[3]).astype(jnp.bfloat16)
    row_count = lax.axis_size("row")
    col_count = lax.axis_size("col")
    devices = row_count * col_count
    hidden = left.shape[0]
    if devices % hidden == 0:
        groups = 1
        copies = devices // hidden
    else:
        groups = hidden // devices
        copies = 1
    share = rows // copies
    left_send = left.reshape(devices, groups * share, cols)
    right_send = jnp.repeat(right, copies, axis=0).reshape(devices, groups, rows, cols)
    left_got, right_got = (
        lax.all_to_all(left_send, ("row", "col"), split_axis=0, concat_axis=0, tiled=True),
        lax.all_to_all(right_send, ("row", "col"), split_axis=0, concat_axis=0, tiled=True),
    )
    left_owned = left_got.reshape(row_count, col_count, groups, share, cols)
    left_owned = left_owned.transpose(2, 0, 3, 1, 4).reshape(
        groups, row_count * share, col_count * cols
    )
    right_owned = right_got.reshape(row_count, col_count, groups, rows, cols)
    right_owned = right_owned.transpose(2, 0, 3, 1, 4).reshape(
        groups, row_count * rows, col_count * cols
    )
    owned_sums = jnp.einsum(
        "gak,gjk->gaj", left_owned, right_owned, preferred_element_type=jnp.float32
    )
    outgoing = owned_sums.reshape(groups, row_count, share, col_count, cols)
    outgoing = outgoing.transpose(1, 3, 0, 2, 4).reshape(devices, groups * share, cols)
    returned = lax.all_to_all(outgoing, ("row", "col"), split_axis=0, concat_axis=0, tiled=True)
    edges = returned.reshape(hidden, rows, cols)
    all_edges = lax.all_gather(edges, "sub", axis=0, tiled=True)
    edgenorm = layer_norm(all_edges, 0).astype(jnp.bfloat16)
    outgate = jax.nn.sigmoid(
        jnp.einsum("ijc,cd->ijd", normed, w_outgate, preferred_element_type=jnp.float32)
    )
    first = pair + outgate * jnp.einsum(
        "hij,hd->ijd", edgenorm, w_outproj, preferred_element_type=jnp.float32
    )
    second = layer_norm(first, -1).astype(jnp.bfloat16)
    attproj = jnp.einsum("ijc,cqe->qije", second, w_attend, preferred_element_type=jnp.float32)
    query = attproj[0].astype(jnp.bfloat16)
    keyed = attproj[1].astype(jnp.bfloat16)
    valued = attproj[2].astype(jnp.bfloat16)
    attgate = attproj[3]
    bias = jnp.einsum("ijc,ch->hij", second, w_bias, preferred_element_type=jnp.float32).astype(
        jnp.bfloat16
    )
    all_keys, all_values = (
        lax.all_gather(keyed, "col", axis=1, tiled=True),
        lax.all_gather(valued, "col", axis=1, tiled=True),
    )
    bias_full = lax.all_gather(bias, "col", axis=2, tiled=True)
    bias_every = lax.all_gather(bias_full, "row", axis=1, tiled=True)
    bias_strip = lax.dynamic_slice_in_dim(bias_every, col_start, cols, 1)
    heads = w_bias.shape[1]
    width = query.shape[2]
    head_size = width // heads
    total = all_keys.shape[1]
    query_heads = query.reshape(rows, cols, heads, head_size)
    key_heads = all_keys.reshape(rows, total, heads, head_size)
    value_heads = all_values.reshape(rows, total, heads, head_size)
    maskbias = 1000000000.0 * (mfloat - 1.0)
    scores = jnp.einsum(
        "ijhd,ikhd->hijk", query_heads, key_heads, preferred_element_type=jnp.float32
    )
    scores = scores / jnp.sqrt(jnp.float32(head_size))
    scores = scores + bias_strip.astype(jnp.float32)[:, None, :, :] + maskbias[None, None, None, :]
    weights = jax.nn.softmax(scores, axis=-1).astype(jnp.bfloat16)
    attended = jnp.einsum(
        "hijk,ikhd->ijhd", weights, value_heads, preferred_element_type=jnp.float32
    )
    mixed = (attended.reshape(rows, cols, width) * jax.nn.sigmoid(attgate)).astype(jnp.bfloat16)
    terms = jnp.einsum("ije,ec->ijc", mixed, w_attout, preferred_element_type=jnp.float32)
    summed = lax.psum(terms.astype(jnp.bfloat16), "sub").astype(jnp.float32)
    return first + summed


def solution(mesh):
    placed = (
        P(("grp", "row"), "col", None),
        P("grp"),
        P(None, None, "sub"),
        P(),
        P(),
        P(None, None, "sub"),
        P(None, "sub"),
        P("sub", None),
    )
    whole = jax.shard_map(
        body, mesh=mesh, in_specs=placed, out_specs=P(("grp", "row"), "col", None), check_vma=False
    )
    if not fits(mesh):
        return whole
    fused = jax.shard_map(
        fused_body, mesh=mesh, in_specs=placed, out_specs=P(("grp", "row"), "col", None), check_vma=False
    )
    parts = mesh.shape["grp"]
    shapes = [
        (128 * parts, 128, 128), (128 * parts,), (128, 4, 128), (128, 128), (128, 128), (128, 4, 128),
        (128, 4), (128, 128),
    ]

    def run(*arrays):
        same = [a.shape for a in arrays] == shapes
        return (fused if same else whole)(*arrays)

    return run
```

```python
import jax
import jax.numpy as jnp
from jax import lax
from jax.experimental import pallas as pl
from jax.experimental.pallas import tpu as pltpu
from jax.sharding import PartitionSpec as P

EPS = 1e-05
MESH = pl.DeviceIdType.MESH
CHUNKS = 1
LOADS = 4


def dot(a, b):
    return jnp.dot(a, b, preferred_element_type=jnp.float32)


def norm_rows(values):
    mean = jnp.mean(values, axis=0, keepdims=True)
    centred = values - mean
    variance = jnp.mean(centred * centred, axis=0, keepdims=True)
    return centred * lax.rsqrt(variance + EPS)


def turned(ref_value):
    return ref_value.astype(jnp.float32).T


def fused_kernel(
    pair_hbm, mask_hbm, we_hbm, wog_hbm, wop_hbm, wa_hbm, wb_hbm, wo_hbm,
    out_ref,
    mask_ref, we_ref, wog_ref, wop_ref, wa_ref, wb_in, wb_ref, wo_ref, scores_t,
    pair_v, wa_all, wb_all, wo_all, sent_l, sent_r, got_l, got_r, wide_l, wide_r, pair_t, normed_t,
    gates, back, owned, wide2,
    first_t, second_t, bias_rows, bias_send, bias_got, bias_t, query_t, keyed, value_t, attgate_t,
    i_sem, p_sem, w_send, w_recv, l_send, l_recv, r_send, r_recv, b_send, b_recv, c_send, c_recv,
    o_send, o_recv,
):
    row = lax.axis_index("row")
    sub = lax.axis_index("sub")
    other = 1 - sub
    side = lax.div(row, 4)
    place = lax.rem(row, 4)
    rows = 16
    half = 8
    step = rows // CHUNKS

    load = rows // LOADS

    def p_copy(c):
        part = pl.ds(c * load, load)
        return pltpu.make_async_copy(pair_hbm.at[part], pair_v.at[part], p_sem.at[c])

    def i_copy(k):
        src, dst = (
            (we_hbm, we_ref), (mask_hbm, mask_ref), (wog_hbm, wog_ref), (wop_hbm, wop_ref),
            (wa_hbm, wa_ref), (wb_hbm, wb_in), (wo_hbm, wo_ref),
        )[k]
        return pltpu.make_async_copy(src, dst, i_sem.at[k])

    p_copy(0).start()
    i_copy(0).start()
    i_copy(1).start()
    for c in range(1, LOADS):
        p_copy(c).start()
    for k in range(2, 7):
        i_copy(k).start()

    def place_to(dg):
        return lax.rem(place + dg, 4)

    def place_from(dg):
        return lax.rem(place + 4 - dg, 4)

    def side_of(ds):
        return side if ds == 0 else 1 - side

    def row_to(ds, dg):
        return side_of(ds) * 4 + place_to(dg)

    def row_from(ds, dg):
        return side_of(ds) * 4 + place_from(dg)

    def peer_sub(d):
        return sub if d == 0 else other

    far = [(1, 3), (1, 2), (1, 1), (1, 0)]
    near = [(0, 3), (0, 2), (0, 1)]
    every = [(ds, dg, d) for ds, dg in far + near for d in (1, 0)] + [(0, 0, 1)]
    around = [(dg, d) for dg in (3, 2, 1) for d in (1, 0)] + [(0, 1)]

    barrier = pltpu.get_barrier_semaphore()
    greeted = [(ds, dg, 0) for ds, dg in far + near] + [(0, 0, 1)]
    for ds, dg, d in greeted:
        pl.semaphore_signal(
            barrier, inc=1, device_id={"row": row_to(ds, dg), "sub": peer_sub(d)}, device_id_type=MESH
        )

    i_copy(0).wait()
    i_copy(1).wait()
    mask_lanes = mask_ref[...].astype(jnp.float32)
    here = lax.broadcasted_iota(jnp.int32, (rows, 128), 1) == (
        row * rows + lax.broadcasted_iota(jnp.int32, (rows, 128), 0)
    )
    mask_rows = jnp.sum(jnp.where(here, mask_lanes, 0.0), axis=1, keepdims=True)
    edge_w = we_ref[...]

    def edge_row(i):
        x = pair_v[i].T
        pair_t[i] = x
        normed = norm_rows(x).astype(jnp.bfloat16)
        normed_t[i] = normed
        projected = dot(edge_w, normed)
        mask_row = mask_lanes * mask_rows[i:i + 1]
        for q, sent in ((0, sent_l), (128, sent_r)):
            edge = mask_row * jax.nn.sigmoid(projected[q:q + 64]) * projected[q + 64:q + 128]
            edge = edge.astype(jnp.bfloat16)
            for g in range(4):
                sent[g, i] = edge[16 * g:16 * g + 16]

    def r_copy(ds, dg, c, slot_from, slot_to):
        part = pl.ds(c * step, step)
        return pltpu.make_async_remote_copy(
            src_ref=sent_r.at[slot_from, part], dst_ref=got_r.at[slot_to, part],
            send_sem=r_send.at[ds * 4 + dg, c], recv_sem=r_recv.at[ds * 4 + dg, c],
            device_id={"row": row_to(ds, dg)}, device_id_type=MESH,
        )

    def l_copy(dg, c, slot_from, slot_to):
        part = pl.ds(c * step, step)
        return pltpu.make_async_remote_copy(
            src_ref=sent_l.at[slot_from, part], dst_ref=got_l.at[slot_to, part],
            send_sem=l_send.at[dg, c], recv_sem=l_recv.at[dg, c],
            device_id={"row": row_to(0, dg)}, device_id_type=MESH,
        )

    def w_copy(k, at):
        src, dst = ((wa_ref, wa_all), (wb_ref, wb_all), (wo_ref, wo_all))[k]
        return pltpu.make_async_remote_copy(
            src_ref=src, dst_ref=dst.at[at], send_sem=w_send.at[k], recv_sem=w_recv.at[k],
            device_id={"sub": other}, device_id_type=MESH,
        )

    for c in range(LOADS):
        p_copy(c).wait()
        for i in range(c * load, (c + 1) * load):
            edge_row(i)
    pl.semaphore_wait(barrier, len(greeted))
    for c in range(CHUNKS):
        for ds, dg in far + near:
            r_copy(ds, dg, c, place_to(dg), row).start()
            if ds == 0:
                l_copy(dg, c, place_to(dg), place).start()
    for k in range(2, 7):
        i_copy(k).wait()
    wb_ref[...] = jnp.concatenate(
        [wb_in[...].astype(jnp.float32), jnp.zeros((14, 128), jnp.float32)], axis=0
    ).astype(jnp.bfloat16)
    for k in range(3):
        w_copy(k, sub).start()

    wa_all[sub] = wa_ref[...]
    wb_all[sub] = wb_ref[...]
    wo_all[sub] = wo_ref[...]
    outgate_t = turned(wog_ref[...]).astype(jnp.bfloat16)
    for i in range(half):
        gates[i] = jax.nn.sigmoid(dot(outgate_t, normed_t[sub * half + i]))
    outproj_t = turned(wop_ref[...]).astype(jnp.bfloat16)

    def widen(dst, at, block):
        dst[pl.ds(pl.multiple_of(at * 256, 256), 256), :] = (
            block.reshape(256, 128).astype(jnp.float32)
        )

    widen(wide_l, place, sent_l[place])
    widen(wide_r, row, sent_r[place])
    for ds, dg in near[::-1] + far[::-1]:
        source = row_from(ds, dg)
        for c in range(CHUNKS):
            r_copy(ds, dg, c, place_to(dg), source).wait_recv()
        widen(wide_r, source, got_r[source])
        if ds == 0:
            for c in range(CHUNKS):
                l_copy(dg, c, place_to(dg), place_from(dg)).wait_recv()
            widen(wide_l, place_from(dg), got_l[place_from(dg)])

    for pair_of in range(8):
        sums = []
        for h in (2 * pair_of, 2 * pair_of + 1):
            left = wide_l[pl.ds(h, 64, stride=16), :].astype(jnp.bfloat16)
            right = wide_r[pl.ds(h, 128, stride=16), :].astype(jnp.bfloat16)
            total = lax.dot_general(
                left, right, (((1,), (1,)), ((), ())), preferred_element_type=jnp.float32
            )
            sums.append(total.reshape(8, 8, 128))
        back[:, pl.ds(16 * pair_of, 16), :] = jnp.concatenate(sums, axis=1).astype(jnp.bfloat16)

    def b_copy(k, dg, d, src, dst):
        return pltpu.make_async_remote_copy(
            src_ref=back.at[src], dst_ref=owned.at[dst], send_sem=b_send.at[k], recv_sem=b_recv.at[k],
            device_id={"row": row_to(0, dg), "sub": peer_sub(d)}, device_id_type=MESH,
        )

    def widen2(at, block):
        wide2[pl.ds(pl.multiple_of(at * 128, 128), 128), :] = block.astype(jnp.float32)

    for k, (dg, d) in enumerate(around):
        b_copy(k, dg, d, place_to(dg) * 2 + peer_sub(d), sub * 4 + place).start()
    widen2(sub * 4 + place, back[place * 2 + sub])

    for k in range(3):
        w_copy(k, other).wait_recv()
    attend_t = jnp.concatenate(
        [wa_all[s, 64 * q:64 * q + 64] for q in range(4) for s in range(2)], axis=0
    )
    bias_w = wb_all[...].reshape(32, 128)
    attout_t = turned(wo_all[...].reshape(128, 128)).astype(jnp.bfloat16)

    for k in reversed(range(len(around))):
        dg, d = around[k]
        source = peer_sub(d) * 4 + place_from(dg)
        b_copy(k, dg, d, 0, source).wait_recv()
        widen2(source, owned[source])

    for i in range(half):
        edgenorm = norm_rows(wide2[pl.ds(i, 128, stride=8), :]).astype(jnp.bfloat16)
        first = pair_t[sub * half + i] + gates[i] * dot(outproj_t, edgenorm)
        first_t[i] = first
        second = norm_rows(first).astype(jnp.bfloat16)
        second_t[i] = second
        bias = dot(bias_w, second)
        for n in range(4):
            r = 16 * (n // 2) + n % 2
            bias_rows[n * 8 + i:n * 8 + i + 1, :] = bias[r:r + 1]
    bias_send[...] = bias_rows[...].astype(jnp.bfloat16)

    def c_copy(k, at):
        ds, dg, d = every[k]
        return pltpu.make_async_remote_copy(
            src_ref=bias_send, dst_ref=bias_got.at[at], send_sem=c_send.at[k], recv_sem=c_recv.at[k],
            device_id={"row": row_to(ds, dg), "sub": peer_sub(d)}, device_id_type=MESH,
        )

    scale = 1.0 / (32.0 ** 0.5)
    mine = row * 2 + sub
    for k in range(len(every)):
        c_copy(k, mine).start()
    bias_got[mine] = bias_send[...]

    for i in range(half):
        projected = dot(attend_t, second_t[i])
        query_t[i] = projected[:128].astype(jnp.bfloat16)
        keyed[i] = projected[128:256].T.astype(jnp.bfloat16)
        value_t[i] = projected[256:384].astype(jnp.bfloat16)
        attgate_t[i] = jax.nn.sigmoid(projected[384:])
    nothing = jnp.zeros((32, 128), jnp.bfloat16)
    for i in range(half):
        query = query_t[i]
        key = keyed[i]
        for n in range(4):
            head = jnp.concatenate(
                [query[32 * m:32 * m + 32] if m == n else nothing for m in range(4)], axis=0
            )
            scores_t[i, n] = dot(key, head) * scale

    for k in reversed(range(len(every))):
        ds, dg, d = every[k]
        c_copy(k, row_from(ds, dg) * 2 + peer_sub(d)).wait_recv()
    maskbias = 1000000000.0 * (mask_lanes - 1.0)
    all_bias = bias_got[...].astype(jnp.float32)
    for n in range(4):
        bias_t[n] = (all_bias[:, n * 8:n * 8 + 8, :].reshape(128, 128) + maskbias).T

    def o_copy(i, at):
        return pltpu.make_async_remote_copy(
            src_ref=out_ref.at[at * half + i], dst_ref=out_ref.at[at * half + i],
            send_sem=o_send.at[i], recv_sem=o_recv.at[i],
            device_id={"sub": other}, device_id_type=MESH,
        )

    def attend_row(i):
        value = value_t[i]
        mixed = []
        for n in range(4):
            scores = scores_t[i, n] + bias_t[n]
            top = jnp.max(scores, axis=0, keepdims=True)
            weights = jnp.exp(scores - top)
            total = jnp.sum(weights, axis=0, keepdims=True)
            mixed.append(dot(value[32 * n:32 * n + 32], weights.astype(jnp.bfloat16)) / total)
        mixed = (jnp.concatenate(mixed, axis=0) * attgate_t[i]).astype(jnp.bfloat16)
        out_ref[sub * half + i] = (first_t[i] + dot(attout_t, mixed)).T

    for i in range(half):
        attend_row(i)
        if i % 2 == 1:
            o_copy(i - 1, sub).start()
            o_copy(i, sub).start()

    for k in range(3):
        w_copy(k, sub).wait_send()
    for c in range(CHUNKS):
        for ds, dg in far + near:
            r_copy(ds, dg, c, place_to(dg), row).wait_send()
            if ds == 0:
                l_copy(dg, c, place_to(dg), place).wait_send()
    for k, (dg, d) in enumerate(around):
        b_copy(k, dg, d, place_to(dg) * 2 + peer_sub(d), sub * 4 + place).wait_send()
    for k in range(len(every)):
        c_copy(k, mine).wait_send()
    for i in range(half):
        o_copy(i, sub).wait_send()
        o_copy(i, other).wait_recv()


def fused_body(pair, mask, w_edges, w_outgate, w_outproj, w_attend, w_bias, w_attout):
    f32, bf16 = jnp.float32, jnp.bfloat16
    vmem = pl.BlockSpec(memory_space=pltpu.VMEM)
    dma = pltpu.SemaphoreType.DMA
    return pl.pallas_call(
        fused_kernel,
        out_shape=jax.ShapeDtypeStruct(pair.shape, f32),
        in_specs=[pl.BlockSpec(memory_space=pltpu.HBM)] * 8,
        out_specs=vmem,
        scratch_shapes=[
            pltpu.VMEM((1, 128), jnp.int32),
            pltpu.VMEM((256, 128), bf16),
            pltpu.VMEM((128, 128), bf16),
            pltpu.VMEM((128, 128), bf16),
            pltpu.VMEM((256, 128), bf16),
            pltpu.VMEM((2, 128), bf16),
            pltpu.VMEM((16, 128), bf16),
            pltpu.VMEM((64, 128), bf16),
            pltpu.VMEM((8, 4, 128, 128), f32),
            pltpu.VMEM((16, 128, 128), f32),
            pltpu.VMEM((2, 256, 128), bf16),
            pltpu.VMEM((2, 16, 128), bf16),
            pltpu.VMEM((2, 64, 128), bf16),
            pltpu.VMEM((4, 16, 16, 128), bf16),
            pltpu.VMEM((4, 16, 16, 128), bf16),
            pltpu.VMEM((4, 16, 16, 128), bf16),
            pltpu.VMEM((8, 16, 16, 128), bf16),
            pltpu.VMEM((1024, 128), f32),
            pltpu.VMEM((2048, 128), f32),
            pltpu.VMEM((16, 128, 128), f32),
            pltpu.VMEM((16, 128, 128), bf16),
            pltpu.VMEM((8, 128, 128), f32),
            pltpu.VMEM((8, 128, 128), bf16),
            pltpu.VMEM((8, 128, 128), bf16),
            pltpu.VMEM((1024, 128), f32),
            pltpu.VMEM((8, 128, 128), f32),
            pltpu.VMEM((8, 128, 128), bf16),
            pltpu.VMEM((32, 128), f32),
            pltpu.VMEM((32, 128), bf16),
            pltpu.VMEM((16, 32, 128), bf16),
            pltpu.VMEM((4, 128, 128), f32),
            pltpu.VMEM((8, 128, 128), bf16),
            pltpu.VMEM((8, 128, 128), bf16),
            pltpu.VMEM((8, 128, 128), bf16),
            pltpu.VMEM((8, 128, 128), f32),
            dma((7,)),
            dma((LOADS,)),
            dma((3,)), dma((3,)),
            dma((4, CHUNKS)), dma((4, CHUNKS)),
            dma((8, CHUNKS)), dma((8, CHUNKS)),
            dma((7,)), dma((7,)),
            dma((15,)), dma((15,)),
            dma((8,)), dma((8,)),
        ],
        compiler_params=pltpu.CompilerParams(
            collective_id=0, has_side_effects=True, vmem_limit_bytes=60 * 1024 * 1024
        ),
        name="window",
    )(
        pair, mask.reshape(1, 128), w_edges.transpose(1, 2, 0).reshape(256, 128), w_outgate,
        w_outproj, w_attend.transpose(1, 2, 0).reshape(256, 128), w_bias.T, w_attout,
    )


def fits(mesh):
    sizes = dict(mesh.shape)
    return sizes["col"] == 1 and sizes["row"] == 8 and sizes["sub"] == 2


def layer_norm(values, axis):
    mean = jnp.mean(values, axis=axis, keepdims=True)
    centred = values - mean
    variance = jnp.mean(centred * centred, axis=axis, keepdims=True)
    return centred * lax.rsqrt(variance + EPS)


def body(pair, mask, w_edges, w_outgate, w_outproj, w_attend, w_bias, w_attout):
    rows, cols, channels = pair.shape
    row_start = lax.axis_index("row") * rows
    col_start = lax.axis_index("col") * cols
    mfloat = mask.astype(jnp.float32)
    mask_rows = lax.dynamic_slice_in_dim(mfloat, row_start, rows, 0)
    mask_cols = lax.dynamic_slice_in_dim(mfloat, col_start, cols, 0)
    pmask = mask_rows[:, None] * mask_cols[None, :]
    normed = layer_norm(pair, -1).astype(jnp.bfloat16)
    projected = jnp.einsum("ijc,cqh->qhij", normed, w_edges, preferred_element_type=jnp.float32)
    left = (pmask * jax.nn.sigmoid(projected[0]) * projected[1]).astype(jnp.bfloat16)
    right = (pmask * jax.nn.sigmoid(projected[2]) * projected[3]).astype(jnp.bfloat16)
    row_count = lax.axis_size("row")
    col_count = lax.axis_size("col")
    devices = row_count * col_count
    hidden = left.shape[0]
    if devices % hidden == 0:
        groups = 1
        copies = devices // hidden
    else:
        groups = hidden // devices
        copies = 1
    share = rows // copies
    left_send = left.reshape(devices, groups * share, cols)
    right_send = jnp.repeat(right, copies, axis=0).reshape(devices, groups, rows, cols)
    left_got, right_got = (
        lax.all_to_all(left_send, ("row", "col"), split_axis=0, concat_axis=0, tiled=True),
        lax.all_to_all(right_send, ("row", "col"), split_axis=0, concat_axis=0, tiled=True),
    )
    left_owned = left_got.reshape(row_count, col_count, groups, share, cols)
    left_owned = left_owned.transpose(2, 0, 3, 1, 4).reshape(
        groups, row_count * share, col_count * cols
    )
    right_owned = right_got.reshape(row_count, col_count, groups, rows, cols)
    right_owned = right_owned.transpose(2, 0, 3, 1, 4).reshape(
        groups, row_count * rows, col_count * cols
    )
    owned_sums = jnp.einsum(
        "gak,gjk->gaj", left_owned, right_owned, preferred_element_type=jnp.float32
    )
    outgoing = owned_sums.reshape(groups, row_count, share, col_count, cols)
    outgoing = outgoing.transpose(1, 3, 0, 2, 4).reshape(devices, groups * share, cols)
    returned = lax.all_to_all(outgoing, ("row", "col"), split_axis=0, concat_axis=0, tiled=True)
    edges = returned.reshape(hidden, rows, cols)
    all_edges = lax.all_gather(edges, "sub", axis=0, tiled=True)
    edgenorm = layer_norm(all_edges, 0).astype(jnp.bfloat16)
    outgate = jax.nn.sigmoid(
        jnp.einsum("ijc,cd->ijd", normed, w_outgate, preferred_element_type=jnp.float32)
    )
    first = pair + outgate * jnp.einsum(
        "hij,hd->ijd", edgenorm, w_outproj, preferred_element_type=jnp.float32
    )
    second = layer_norm(first, -1).astype(jnp.bfloat16)
    attproj = jnp.einsum("ijc,cqe->qije", second, w_attend, preferred_element_type=jnp.float32)
    query = attproj[0].astype(jnp.bfloat16)
    keyed = attproj[1].astype(jnp.bfloat16)
    valued = attproj[2].astype(jnp.bfloat16)
    attgate = attproj[3]
    bias = jnp.einsum("ijc,ch->hij", second, w_bias, preferred_element_type=jnp.float32).astype(
        jnp.bfloat16
    )
    all_keys, all_values = (
        lax.all_gather(keyed, "col", axis=1, tiled=True),
        lax.all_gather(valued, "col", axis=1, tiled=True),
    )
    bias_full = lax.all_gather(bias, "col", axis=2, tiled=True)
    bias_every = lax.all_gather(bias_full, "row", axis=1, tiled=True)
    bias_strip = lax.dynamic_slice_in_dim(bias_every, col_start, cols, 1)
    heads = w_bias.shape[1]
    width = query.shape[2]
    head_size = width // heads
    total = all_keys.shape[1]
    query_heads = query.reshape(rows, cols, heads, head_size)
    key_heads = all_keys.reshape(rows, total, heads, head_size)
    value_heads = all_values.reshape(rows, total, heads, head_size)
    maskbias = 1000000000.0 * (mfloat - 1.0)
    scores = jnp.einsum(
        "ijhd,ikhd->hijk", query_heads, key_heads, preferred_element_type=jnp.float32
    )
    scores = scores / jnp.sqrt(jnp.float32(head_size))
    scores = scores + bias_strip.astype(jnp.float32)[:, None, :, :] + maskbias[None, None, None, :]
    weights = jax.nn.softmax(scores, axis=-1).astype(jnp.bfloat16)
    attended = jnp.einsum(
        "hijk,ikhd->ijhd", weights, value_heads, preferred_element_type=jnp.float32
    )
    mixed = (attended.reshape(rows, cols, width) * jax.nn.sigmoid(attgate)).astype(jnp.bfloat16)
    terms = jnp.einsum("ije,ec->ijc", mixed, w_attout, preferred_element_type=jnp.float32)
    summed = lax.psum(terms.astype(jnp.bfloat16), "sub").astype(jnp.float32)
    return first + summed


def solution(mesh):
    placed = (
        P(("grp", "row"), "col", None),
        P("grp"),
        P(None, None, "sub"),
        P(),
        P(),
        P(None, None, "sub"),
        P(None, "sub"),
        P("sub", None),
    )
    whole = jax.shard_map(
        body, mesh=mesh, in_specs=placed, out_specs=P(("grp", "row"), "col", None), check_vma=False
    )
    if not fits(mesh):
        return whole
    fused = jax.shard_map(
        fused_body, mesh=mesh, in_specs=placed, out_specs=P(("grp", "row"), "col", None), check_vma=False
    )
    parts = mesh.shape["grp"]
    shapes = [
        (128 * parts, 128, 128), (128 * parts,), (128, 4, 128), (128, 128), (128, 128), (128, 4, 128),
        (128, 4), (128, 128),
    ]

    def run(*arrays):
        same = [a.shape for a in arrays] == shapes
        return (fused if same else whole)(*arrays)

    return run
```

```python
import jax
import jax.numpy as jnp
from jax import lax
from jax.experimental import pallas as pl
from jax.experimental.pallas import tpu as pltpu
from jax.sharding import PartitionSpec as P

EPS = 1e-05
MESH = pl.DeviceIdType.MESH
CHUNKS = 1
LOADS = 4


def dot(a, b):
    return jnp.dot(a, b, preferred_element_type=jnp.float32)


def norm_rows(values):
    mean = jnp.mean(values, axis=0, keepdims=True)
    centred = values - mean
    variance = jnp.mean(centred * centred, axis=0, keepdims=True)
    return centred * lax.rsqrt(variance + EPS)


def turned(ref_value):
    return ref_value.astype(jnp.float32).T


def fused_kernel(
    pair_hbm, mask_hbm, we_hbm, wog_hbm, wop_hbm, wa_hbm, wb_hbm, wo_hbm,
    out_ref,
    mask_ref, we_ref, wog_ref, wop_ref, wa_ref, wb_in, wb_ref, wo_ref, scores_t,
    pair_v, wa_all, wb_all, wo_all, sent_l, sent_r, got_l, got_r, wide_l, wide_r, pair_t, normed_t,
    gates, back, owned, wide2,
    change_t, second_t, bias_rows, bias_send, bias_got, bias_t, query_t, keyed, value_t, attgate_t,
    i_sem, p_sem, w_send, w_recv, l_send, l_recv, r_send, r_recv, b_send, b_recv, c_send, c_recv,
    o_send, o_recv, own_sem, out_v,
):
    row = lax.axis_index("row")
    sub = lax.axis_index("sub")
    other = 1 - sub
    side = lax.div(row, 4)
    place = lax.rem(row, 4)
    rows = 16
    half = 8
    step = rows // CHUNKS

    load = rows // LOADS

    def p_copy(c):
        part = pl.ds(c * load, load)
        return pltpu.make_async_copy(pair_hbm.at[part], pair_v.at[part], p_sem.at[c])

    def i_copy(k):
        src, dst = (
            (we_hbm, we_ref), (mask_hbm, mask_ref), (wog_hbm, wog_ref), (wop_hbm, wop_ref),
            (wa_hbm, wa_ref), (wb_hbm, wb_in), (wo_hbm, wo_ref),
        )[k]
        return pltpu.make_async_copy(src, dst, i_sem.at[k])

    p_copy(0).start()
    i_copy(0).start()
    i_copy(1).start()
    for c in range(1, LOADS):
        p_copy(c).start()
    for k in range(2, 7):
        i_copy(k).start()

    def place_to(dg):
        return lax.rem(place + dg, 4)

    def place_from(dg):
        return lax.rem(place + 4 - dg, 4)

    def side_of(ds):
        return side if ds == 0 else 1 - side

    def row_to(ds, dg):
        return side_of(ds) * 4 + place_to(dg)

    def row_from(ds, dg):
        return side_of(ds) * 4 + place_from(dg)

    def peer_sub(d):
        return sub if d == 0 else other

    far = [(1, 3), (1, 2), (1, 1), (1, 0)]
    near = [(0, 3), (0, 2), (0, 1)]
    every = [(ds, dg, d) for ds, dg in far + near for d in (1, 0)] + [(0, 0, 1)]
    around = [(dg, d) for dg in (3, 2, 1) for d in (1, 0)] + [(0, 1)]

    barrier = pltpu.get_barrier_semaphore()
    greeted = [(ds, dg, 0) for ds, dg in far + near] + [(0, 0, 1)]
    for ds, dg, d in greeted:
        pl.semaphore_signal(
            barrier, inc=1, device_id={"row": row_to(ds, dg), "sub": peer_sub(d)}, device_id_type=MESH
        )

    i_copy(0).wait()
    i_copy(1).wait()
    mask_lanes = mask_ref[...].astype(jnp.float32)
    here = lax.broadcasted_iota(jnp.int32, (rows, 128), 1) == (
        row * rows + lax.broadcasted_iota(jnp.int32, (rows, 128), 0)
    )
    mask_rows = jnp.sum(jnp.where(here, mask_lanes, 0.0), axis=1, keepdims=True)
    edge_w = we_ref[...]

    def edge_row(i):
        x = pair_v[i].T
        pair_t[i] = x
        normed = norm_rows(x).astype(jnp.bfloat16)
        normed_t[i] = normed
        projected = dot(edge_w, normed)
        mask_row = mask_lanes * mask_rows[i:i + 1]
        for q, sent in ((0, sent_l), (128, sent_r)):
            edge = mask_row * jax.nn.sigmoid(projected[q:q + 64]) * projected[q + 64:q + 128]
            edge = edge.astype(jnp.bfloat16)
            for g in range(4):
                sent[g, i] = edge[16 * g:16 * g + 16]

    def r_copy(ds, dg, c, slot_from, slot_to):
        part = pl.ds(c * step, step)
        return pltpu.make_async_remote_copy(
            src_ref=sent_r.at[slot_from, part], dst_ref=got_r.at[slot_to, part],
            send_sem=r_send.at[ds * 4 + dg, c], recv_sem=r_recv.at[ds * 4 + dg, c],
            device_id={"row": row_to(ds, dg)}, device_id_type=MESH,
        )

    def l_copy(dg, c, slot_from, slot_to):
        part = pl.ds(c * step, step)
        return pltpu.make_async_remote_copy(
            src_ref=sent_l.at[slot_from, part], dst_ref=got_l.at[slot_to, part],
            send_sem=l_send.at[dg, c], recv_sem=l_recv.at[dg, c],
            device_id={"row": row_to(0, dg)}, device_id_type=MESH,
        )

    def w_copy(k, at):
        src, dst = ((wa_ref, wa_all), (wb_ref, wb_all), (wo_ref, wo_all))[k]
        return pltpu.make_async_remote_copy(
            src_ref=src, dst_ref=dst.at[at], send_sem=w_send.at[k], recv_sem=w_recv.at[k],
            device_id={"sub": other}, device_id_type=MESH,
        )

    for c in range(LOADS):
        p_copy(c).wait()
        for i in range(c * load, (c + 1) * load):
            edge_row(i)
    pl.semaphore_wait(barrier, len(greeted))
    for c in range(CHUNKS):
        for ds, dg in far + near:
            r_copy(ds, dg, c, place_to(dg), row).start()
            if ds == 0:
                l_copy(dg, c, place_to(dg), place).start()
    for k in range(2, 7):
        i_copy(k).wait()
    wb_ref[...] = jnp.concatenate(
        [wb_in[...].astype(jnp.float32), jnp.zeros((14, 128), jnp.float32)], axis=0
    ).astype(jnp.bfloat16)
    for k in range(3):
        w_copy(k, sub).start()

    wa_all[sub] = wa_ref[...]
    wb_all[sub] = wb_ref[...]
    wo_all[sub] = wo_ref[...]
    outgate_t = turned(wog_ref[...]).astype(jnp.bfloat16)
    for i in range(half):
        gates[i] = jax.nn.sigmoid(dot(outgate_t, normed_t[sub * half + i]))
    outproj_t = turned(wop_ref[...]).astype(jnp.bfloat16)

    def widen(dst, at, block):
        dst[pl.ds(pl.multiple_of(at * 256, 256), 256), :] = (
            block.reshape(256, 128).astype(jnp.float32)
        )

    widen(wide_l, place, sent_l[place])
    widen(wide_r, row, sent_r[place])
    for ds, dg in near[::-1] + far[::-1]:
        source = row_from(ds, dg)
        for c in range(CHUNKS):
            r_copy(ds, dg, c, place_to(dg), source).wait_recv()
        widen(wide_r, source, got_r[source])
        if ds == 0:
            for c in range(CHUNKS):
                l_copy(dg, c, place_to(dg), place_from(dg)).wait_recv()
            widen(wide_l, place_from(dg), got_l[place_from(dg)])

    for pair_of in range(8):
        sums = []
        for h in (2 * pair_of, 2 * pair_of + 1):
            left = wide_l[pl.ds(h, 64, stride=16), :].astype(jnp.bfloat16)
            right = wide_r[pl.ds(h, 128, stride=16), :].astype(jnp.bfloat16)
            total = lax.dot_general(
                left, right, (((1,), (1,)), ((), ())), preferred_element_type=jnp.float32
            )
            sums.append(total.reshape(8, 8, 128))
        back[:, pl.ds(16 * pair_of, 16), :] = jnp.concatenate(sums, axis=1).astype(jnp.bfloat16)

    def b_copy(k, dg, d, src, dst):
        return pltpu.make_async_remote_copy(
            src_ref=back.at[src], dst_ref=owned.at[dst], send_sem=b_send.at[k], recv_sem=b_recv.at[k],
            device_id={"row": row_to(0, dg), "sub": peer_sub(d)}, device_id_type=MESH,
        )

    def widen2(at, block):
        wide2[pl.ds(pl.multiple_of(at * 128, 128), 128), :] = block.astype(jnp.float32)

    for k, (dg, d) in enumerate(around):
        b_copy(k, dg, d, place_to(dg) * 2 + peer_sub(d), sub * 4 + place).start()
    widen2(sub * 4 + place, back[place * 2 + sub])

    for k in range(3):
        w_copy(k, other).wait_recv()
    attend_t = jnp.concatenate(
        [wa_all[s, 64 * q:64 * q + 64] for q in range(4) for s in range(2)], axis=0
    )
    bias_w = wb_all[...].reshape(32, 128)
    attout_t = turned(wo_all[...].reshape(128, 128)).astype(jnp.bfloat16)

    for k in reversed(range(len(around))):
        dg, d = around[k]
        source = peer_sub(d) * 4 + place_from(dg)
        b_copy(k, dg, d, 0, source).wait_recv()
        widen2(source, owned[source])

    for i in range(half):
        edgenorm = norm_rows(wide2[pl.ds(i, 128, stride=8), :]).astype(jnp.bfloat16)
        change = gates[i] * dot(outproj_t, edgenorm)
        change_t[i] = change
        first = pair_t[sub * half + i] + change
        second = norm_rows(first).astype(jnp.bfloat16)
        second_t[i] = second
        bias = dot(bias_w, second)
        for n in range(4):
            r = 16 * (n // 2) + n % 2
            bias_rows[n * 8 + i:n * 8 + i + 1, :] = bias[r:r + 1]
    bias_send[...] = bias_rows[...].astype(jnp.bfloat16)

    def c_copy(k, at):
        ds, dg, d = every[k]
        return pltpu.make_async_remote_copy(
            src_ref=bias_send, dst_ref=bias_got.at[at], send_sem=c_send.at[k], recv_sem=c_recv.at[k],
            device_id={"row": row_to(ds, dg), "sub": peer_sub(d)}, device_id_type=MESH,
        )

    scale = 1.0 / (32.0 ** 0.5)
    mine = row * 2 + sub
    for k in range(len(every)):
        c_copy(k, mine).start()
    bias_got[mine] = bias_send[...]

    for i in range(half):
        projected = dot(attend_t, second_t[i])
        query_t[i] = projected[:128].astype(jnp.bfloat16)
        keyed[i] = projected[128:256].T.astype(jnp.bfloat16)
        value_t[i] = projected[256:384].astype(jnp.bfloat16)
        attgate_t[i] = jax.nn.sigmoid(projected[384:])
    nothing = jnp.zeros((32, 128), jnp.bfloat16)
    for i in range(half):
        query = query_t[i]
        key = keyed[i]
        for n in range(4):
            head = jnp.concatenate(
                [query[32 * m:32 * m + 32] if m == n else nothing for m in range(4)], axis=0
            )
            scores_t[i, n] = dot(key, head) * scale

    for k in reversed(range(len(every))):
        ds, dg, d = every[k]
        c_copy(k, row_from(ds, dg) * 2 + peer_sub(d)).wait_recv()
    maskbias = 1000000000.0 * (mask_lanes - 1.0)
    all_bias = bias_got[...].astype(jnp.float32)
    for n in range(4):
        bias_t[n] = (all_bias[:, n * 8:n * 8 + 8, :].reshape(128, 128) + maskbias).T

    def o_copy(i, at):
        return pltpu.make_async_remote_copy(
            src_ref=out_v.at[i], dst_ref=out_ref.at[at * half + i],
            send_sem=o_send.at[i], recv_sem=o_recv.at[i],
            device_id={"sub": other}, device_id_type=MESH,
        )

    def own_copy(i):
        return pltpu.make_async_copy(out_v.at[i], out_ref.at[sub * half + i], own_sem.at[i])

    def attend_row(i):
        value = value_t[i]
        mixed = []
        for n in range(4):
            scores = scores_t[i, n] + bias_t[n]
            top = jnp.max(scores, axis=0, keepdims=True)
            weights = jnp.exp(scores - top)
            total = jnp.sum(weights, axis=0, keepdims=True)
            mixed.append(dot(value[32 * n:32 * n + 32], weights.astype(jnp.bfloat16)) / total)
        mixed = (jnp.concatenate(mixed, axis=0) * attgate_t[i]).astype(jnp.bfloat16)
        out_v[i] = (change_t[i] + dot(attout_t, mixed)).T

    for i in range(half):
        attend_row(i)
        if i % 2 == 1:
            o_copy(i - 1, sub).start()
            o_copy(i, sub).start()
            own_copy(i - 1).start()
            own_copy(i).start()

    for k in range(3):
        w_copy(k, sub).wait_send()
    for c in range(CHUNKS):
        for ds, dg in far + near:
            r_copy(ds, dg, c, place_to(dg), row).wait_send()
            if ds == 0:
                l_copy(dg, c, place_to(dg), place).wait_send()
    for k, (dg, d) in enumerate(around):
        b_copy(k, dg, d, place_to(dg) * 2 + peer_sub(d), sub * 4 + place).wait_send()
    for k in range(len(every)):
        c_copy(k, mine).wait_send()
    for i in range(half):
        own_copy(i).wait()
        o_copy(i, sub).wait_send()
        o_copy(i, other).wait_recv()


def fused_body(pair, mask, w_edges, w_outgate, w_outproj, w_attend, w_bias, w_attout):
    f32, bf16 = jnp.float32, jnp.bfloat16
    dma = pltpu.SemaphoreType.DMA
    change = pl.pallas_call(
        fused_kernel,
        out_shape=jax.ShapeDtypeStruct(pair.shape, f32),
        in_specs=[pl.BlockSpec(memory_space=pltpu.HBM)] * 8,
        out_specs=pl.BlockSpec(memory_space=pltpu.HBM),
        scratch_shapes=[
            pltpu.VMEM((1, 128), jnp.int32),
            pltpu.VMEM((256, 128), bf16),
            pltpu.VMEM((128, 128), bf16),
            pltpu.VMEM((128, 128), bf16),
            pltpu.VMEM((256, 128), bf16),
            pltpu.VMEM((2, 128), bf16),
            pltpu.VMEM((16, 128), bf16),
            pltpu.VMEM((64, 128), bf16),
            pltpu.VMEM((8, 4, 128, 128), f32),
            pltpu.VMEM((16, 128, 128), f32),
            pltpu.VMEM((2, 256, 128), bf16),
            pltpu.VMEM((2, 16, 128), bf16),
            pltpu.VMEM((2, 64, 128), bf16),
            pltpu.VMEM((4, 16, 16, 128), bf16),
            pltpu.VMEM((4, 16, 16, 128), bf16),
            pltpu.VMEM((4, 16, 16, 128), bf16),
            pltpu.VMEM((8, 16, 16, 128), bf16),
            pltpu.VMEM((1024, 128), f32),
            pltpu.VMEM((2048, 128), f32),
            pltpu.VMEM((16, 128, 128), f32),
            pltpu.VMEM((16, 128, 128), bf16),
            pltpu.VMEM((8, 128, 128), f32),
            pltpu.VMEM((8, 128, 128), bf16),
            pltpu.VMEM((8, 128, 128), bf16),
            pltpu.VMEM((1024, 128), f32),
            pltpu.VMEM((8, 128, 128), f32),
            pltpu.VMEM((8, 128, 128), bf16),
            pltpu.VMEM((32, 128), f32),
            pltpu.VMEM((32, 128), bf16),
            pltpu.VMEM((16, 32, 128), bf16),
            pltpu.VMEM((4, 128, 128), f32),
            pltpu.VMEM((8, 128, 128), bf16),
            pltpu.VMEM((8, 128, 128), bf16),
            pltpu.VMEM((8, 128, 128), bf16),
            pltpu.VMEM((8, 128, 128), f32),
            dma((7,)),
            dma((LOADS,)),
            dma((3,)), dma((3,)),
            dma((4, CHUNKS)), dma((4, CHUNKS)),
            dma((8, CHUNKS)), dma((8, CHUNKS)),
            dma((7,)), dma((7,)),
            dma((15,)), dma((15,)),
            dma((8,)), dma((8,)), dma((8,)),
            pltpu.VMEM((8, 128, 128), f32),
        ],
        compiler_params=pltpu.CompilerParams(
            collective_id=0, has_side_effects=True, vmem_limit_bytes=60 * 1024 * 1024
        ),
        name="window",
    )(
        pair, mask.reshape(1, 128), w_edges.transpose(1, 2, 0).reshape(256, 128), w_outgate,
        w_outproj, w_attend.transpose(1, 2, 0).reshape(256, 128), w_bias.T, w_attout,
    )
    return pair + change


def fits(mesh):
    sizes = dict(mesh.shape)
    return sizes["col"] == 1 and sizes["row"] == 8 and sizes["sub"] == 2


def layer_norm(values, axis):
    mean = jnp.mean(values, axis=axis, keepdims=True)
    centred = values - mean
    variance = jnp.mean(centred * centred, axis=axis, keepdims=True)
    return centred * lax.rsqrt(variance + EPS)


def body(pair, mask, w_edges, w_outgate, w_outproj, w_attend, w_bias, w_attout):
    rows, cols, channels = pair.shape
    row_start = lax.axis_index("row") * rows
    col_start = lax.axis_index("col") * cols
    mfloat = mask.astype(jnp.float32)
    mask_rows = lax.dynamic_slice_in_dim(mfloat, row_start, rows, 0)
    mask_cols = lax.dynamic_slice_in_dim(mfloat, col_start, cols, 0)
    pmask = mask_rows[:, None] * mask_cols[None, :]
    normed = layer_norm(pair, -1).astype(jnp.bfloat16)
    projected = jnp.einsum("ijc,cqh->qhij", normed, w_edges, preferred_element_type=jnp.float32)
    left = (pmask * jax.nn.sigmoid(projected[0]) * projected[1]).astype(jnp.bfloat16)
    right = (pmask * jax.nn.sigmoid(projected[2]) * projected[3]).astype(jnp.bfloat16)
    row_count = lax.axis_size("row")
    col_count = lax.axis_size("col")
    devices = row_count * col_count
    hidden = left.shape[0]
    if devices % hidden == 0:
        groups = 1
        copies = devices // hidden
    else:
        groups = hidden // devices
        copies = 1
    share = rows // copies
    left_send = left.reshape(devices, groups * share, cols)
    right_send = jnp.repeat(right, copies, axis=0).reshape(devices, groups, rows, cols)
    left_got, right_got = (
        lax.all_to_all(left_send, ("row", "col"), split_axis=0, concat_axis=0, tiled=True),
        lax.all_to_all(right_send, ("row", "col"), split_axis=0, concat_axis=0, tiled=True),
    )
    left_owned = left_got.reshape(row_count, col_count, groups, share, cols)
    left_owned = left_owned.transpose(2, 0, 3, 1, 4).reshape(
        groups, row_count * share, col_count * cols
    )
    right_owned = right_got.reshape(row_count, col_count, groups, rows, cols)
    right_owned = right_owned.transpose(2, 0, 3, 1, 4).reshape(
        groups, row_count * rows, col_count * cols
    )
    owned_sums = jnp.einsum(
        "gak,gjk->gaj", left_owned, right_owned, preferred_element_type=jnp.float32
    )
    outgoing = owned_sums.reshape(groups, row_count, share, col_count, cols)
    outgoing = outgoing.transpose(1, 3, 0, 2, 4).reshape(devices, groups * share, cols)
    returned = lax.all_to_all(outgoing, ("row", "col"), split_axis=0, concat_axis=0, tiled=True)
    edges = returned.reshape(hidden, rows, cols)
    all_edges = lax.all_gather(edges, "sub", axis=0, tiled=True)
    edgenorm = layer_norm(all_edges, 0).astype(jnp.bfloat16)
    outgate = jax.nn.sigmoid(
        jnp.einsum("ijc,cd->ijd", normed, w_outgate, preferred_element_type=jnp.float32)
    )
    first = pair + outgate * jnp.einsum(
        "hij,hd->ijd", edgenorm, w_outproj, preferred_element_type=jnp.float32
    )
    second = layer_norm(first, -1).astype(jnp.bfloat16)
    attproj = jnp.einsum("ijc,cqe->qije", second, w_attend, preferred_element_type=jnp.float32)
    query = attproj[0].astype(jnp.bfloat16)
    keyed = attproj[1].astype(jnp.bfloat16)
    valued = attproj[2].astype(jnp.bfloat16)
    attgate = attproj[3]
    bias = jnp.einsum("ijc,ch->hij", second, w_bias, preferred_element_type=jnp.float32).astype(
        jnp.bfloat16
    )
    all_keys, all_values = (
        lax.all_gather(keyed, "col", axis=1, tiled=True),
        lax.all_gather(valued, "col", axis=1, tiled=True),
    )
    bias_full = lax.all_gather(bias, "col", axis=2, tiled=True)
    bias_every = lax.all_gather(bias_full, "row", axis=1, tiled=True)
    bias_strip = lax.dynamic_slice_in_dim(bias_every, col_start, cols, 1)
    heads = w_bias.shape[1]
    width = query.shape[2]
    head_size = width // heads
    total = all_keys.shape[1]
    query_heads = query.reshape(rows, cols, heads, head_size)
    key_heads = all_keys.reshape(rows, total, heads, head_size)
    value_heads = all_values.reshape(rows, total, heads, head_size)
    maskbias = 1000000000.0 * (mfloat - 1.0)
    scores = jnp.einsum(
        "ijhd,ikhd->hijk", query_heads, key_heads, preferred_element_type=jnp.float32
    )
    scores = scores / jnp.sqrt(jnp.float32(head_size))
    scores = scores + bias_strip.astype(jnp.float32)[:, None, :, :] + maskbias[None, None, None, :]
    weights = jax.nn.softmax(scores, axis=-1).astype(jnp.bfloat16)
    attended = jnp.einsum(
        "hijk,ikhd->ijhd", weights, value_heads, preferred_element_type=jnp.float32
    )
    mixed = (attended.reshape(rows, cols, width) * jax.nn.sigmoid(attgate)).astype(jnp.bfloat16)
    terms = jnp.einsum("ije,ec->ijc", mixed, w_attout, preferred_element_type=jnp.float32)
    summed = lax.psum(terms.astype(jnp.bfloat16), "sub").astype(jnp.float32)
    return first + summed


def solution(mesh):
    placed = (
        P(("grp", "row"), "col", None),
        P("grp"),
        P(None, None, "sub"),
        P(),
        P(),
        P(None, None, "sub"),
        P(None, "sub"),
        P("sub", None),
    )
    whole = jax.shard_map(
        body, mesh=mesh, in_specs=placed, out_specs=P(("grp", "row"), "col", None), check_vma=False
    )
    if not fits(mesh):
        return whole
    fused = jax.shard_map(
        fused_body, mesh=mesh, in_specs=placed, out_specs=P(("grp", "row"), "col", None), check_vma=False
    )
    parts = mesh.shape["grp"]
    shapes = [
        (128 * parts, 128, 128), (128 * parts,), (128, 4, 128), (128, 128), (128, 128), (128, 4, 128),
        (128, 4), (128, 128),
    ]

    def run(*arrays):
        same = [a.shape for a in arrays] == shapes
        return (fused if same else whole)(*arrays)

    return run
```

```python
import jax
import jax.numpy as jnp
from jax import lax
from jax.experimental import pallas as pl
from jax.experimental.pallas import tpu as pltpu
from jax.sharding import PartitionSpec as P

EPS = 1e-05
MESH = pl.DeviceIdType.MESH
CHUNKS = 1
LOADS = 4


def dot(a, b):
    return jnp.dot(a, b, preferred_element_type=jnp.float32)


def norm_rows(values):
    mean = jnp.mean(values, axis=0, keepdims=True)
    centred = values - mean
    variance = jnp.mean(centred * centred, axis=0, keepdims=True)
    return centred * lax.rsqrt(variance + EPS)


def turned(ref_value):
    return ref_value.astype(jnp.float32).T


def fused_kernel(
    pair_hbm, mask_hbm, we_hbm, wog_hbm, wop_hbm, wa_hbm, wb_hbm, wo_hbm,
    out_ref,
    mask_ref, we_ref, wog_ref, wop_ref, wa_ref, wb_in, wb_ref, wo_ref, scores_t,
    pair_v, wa_all, wb_all, wo_all, sent_l, sent_r, got_l, got_r, wide_l, wide_r, pair_t, normed_t,
    gates, back, owned, wide2,
    change_t, second_t, bias_rows, bias_send, bias_got, bias_t, query_t, keyed, value_t, attgate_t,
    i_sem, p_sem, w_send, w_recv, l_send, l_recv, r_send, r_recv, b_send, b_recv, c_send, c_recv,
    o_send, o_recv, own_sem, out_v,
):
    row = lax.axis_index("row")
    sub = lax.axis_index("sub")
    other = 1 - sub
    side = lax.div(row, 4)
    place = lax.rem(row, 4)
    rows = 16
    half = 8
    step = rows // CHUNKS

    load = rows // LOADS

    def p_copy(c):
        part = pl.ds(c * load, load)
        return pltpu.make_async_copy(pair_hbm.at[part], pair_v.at[part], p_sem.at[c])

    def i_copy(k):
        src, dst = (
            (we_hbm, we_ref), (mask_hbm, mask_ref), (wog_hbm, wog_ref), (wop_hbm, wop_ref),
            (wa_hbm, wa_ref), (wb_hbm, wb_in), (wo_hbm, wo_ref),
        )[k]
        return pltpu.make_async_copy(src, dst, i_sem.at[k])

    p_copy(0).start()
    i_copy(0).start()
    i_copy(1).start()
    for c in range(1, LOADS):
        p_copy(c).start()
    for k in range(2, 7):
        i_copy(k).start()

    def place_to(dg):
        return lax.rem(place + dg, 4)

    def place_from(dg):
        return lax.rem(place + 4 - dg, 4)

    def side_of(ds):
        return side if ds == 0 else 1 - side

    def row_to(ds, dg):
        return side_of(ds) * 4 + place_to(dg)

    def row_from(ds, dg):
        return side_of(ds) * 4 + place_from(dg)

    def peer_sub(d):
        return sub if d == 0 else other

    far = [(1, 3), (1, 2), (1, 1), (1, 0)]
    near = [(0, 3), (0, 2), (0, 1)]
    every = [(ds, dg, d) for ds, dg in far + near for d in (1, 0)] + [(0, 0, 1)]
    around = [(dg, d) for dg in (3, 2, 1) for d in (1, 0)] + [(0, 1)]

    barrier = pltpu.get_barrier_semaphore()
    greeted = [(ds, dg, 0) for ds, dg in far + near] + [(0, 0, 1)]
    for ds, dg, d in greeted:
        pl.semaphore_signal(
            barrier, inc=1, device_id={"row": row_to(ds, dg), "sub": peer_sub(d)}, device_id_type=MESH
        )

    i_copy(0).wait()
    i_copy(1).wait()
    mask_lanes = mask_ref[...].astype(jnp.float32)
    here = lax.broadcasted_iota(jnp.int32, (rows, 128), 1) == (
        row * rows + lax.broadcasted_iota(jnp.int32, (rows, 128), 0)
    )
    mask_rows = jnp.sum(jnp.where(here, mask_lanes, 0.0), axis=1, keepdims=True)
    edge_w = we_ref[...]

    def edge_row(i):
        x = pair_v[i].T
        pair_t[i] = x
        normed = norm_rows(x).astype(jnp.bfloat16)
        normed_t[i] = normed
        projected = dot(edge_w, normed)
        mask_row = mask_lanes * mask_rows[i:i + 1]
        for q, sent in ((0, sent_l), (128, sent_r)):
            edge = mask_row * jax.nn.sigmoid(projected[q:q + 64]) * projected[q + 64:q + 128]
            edge = edge.astype(jnp.bfloat16)
            for g in range(4):
                sent[g, i] = edge[16 * g:16 * g + 16]

    def r_copy(ds, dg, c, slot_from, slot_to):
        part = pl.ds(c * step, step)
        return pltpu.make_async_remote_copy(
            src_ref=sent_r.at[slot_from, part], dst_ref=got_r.at[slot_to, part],
            send_sem=r_send.at[ds * 4 + dg, c], recv_sem=r_recv.at[ds * 4 + dg, c],
            device_id={"row": row_to(ds, dg)}, device_id_type=MESH,
        )

    def l_copy(dg, c, slot_from, slot_to):
        part = pl.ds(c * step, step)
        return pltpu.make_async_remote_copy(
            src_ref=sent_l.at[slot_from, part], dst_ref=got_l.at[slot_to, part],
            send_sem=l_send.at[dg, c], recv_sem=l_recv.at[dg, c],
            device_id={"row": row_to(0, dg)}, device_id_type=MESH,
        )

    def w_copy(k, at):
        src, dst = ((wa_ref, wa_all), (wb_ref, wb_all), (wo_ref, wo_all))[k]
        return pltpu.make_async_remote_copy(
            src_ref=src, dst_ref=dst.at[at], send_sem=w_send.at[k], recv_sem=w_recv.at[k],
            device_id={"sub": other}, device_id_type=MESH,
        )

    for c in range(LOADS):
        p_copy(c).wait()
        for i in range(c * load, (c + 1) * load):
            edge_row(i)
    pl.semaphore_wait(barrier, len(greeted))
    for c in range(CHUNKS):
        for ds, dg in far + near:
            r_copy(ds, dg, c, place_to(dg), row).start()
            if ds == 0:
                l_copy(dg, c, place_to(dg), place).start()
    for k in range(2, 7):
        i_copy(k).wait()
    wb_ref[...] = jnp.concatenate(
        [wb_in[...].astype(jnp.float32), jnp.zeros((14, 128), jnp.float32)], axis=0
    ).astype(jnp.bfloat16)
    for k in range(3):
        w_copy(k, sub).start()

    wa_all[sub] = wa_ref[...]
    wb_all[sub] = wb_ref[...]
    wo_all[sub] = wo_ref[...]
    outgate_t = turned(wog_ref[...]).astype(jnp.bfloat16)
    for i in range(half):
        gates[i] = jax.nn.sigmoid(dot(outgate_t, normed_t[sub * half + i]))
    outproj_t = turned(wop_ref[...]).astype(jnp.bfloat16)

    def widen(dst, at, block):
        dst[pl.ds(pl.multiple_of(at * 256, 256), 256), :] = (
            block.reshape(256, 128).astype(jnp.float32)
        )

    widen(wide_l, place, sent_l[place])
    widen(wide_r, row, sent_r[place])
    for ds, dg in near[::-1] + far[::-1]:
        source = row_from(ds, dg)
        for c in range(CHUNKS):
            r_copy(ds, dg, c, place_to(dg), source).wait_recv()
        widen(wide_r, source, got_r[source])
        if ds == 0:
            for c in range(CHUNKS):
                l_copy(dg, c, place_to(dg), place_from(dg)).wait_recv()
            widen(wide_l, place_from(dg), got_l[place_from(dg)])

    def b_copy(k, q, src, dst):
        dg, d = around[k]
        part = pl.ds(64 * q, 64)
        return pltpu.make_async_remote_copy(
            src_ref=back.at[src, part], dst_ref=owned.at[dst, part],
            send_sem=b_send.at[k, q], recv_sem=b_recv.at[k, q],
            device_id={"row": row_to(0, dg), "sub": peer_sub(d)}, device_id_type=MESH,
        )

    def b_part(k, q):
        dg, d = around[k]
        return b_copy(k, q, place_to(dg) * 2 + peer_sub(d), sub * 4 + place)

    for pair_of in range(8):
        sums = []
        for h in (2 * pair_of, 2 * pair_of + 1):
            left = wide_l[pl.ds(h, 64, stride=16), :].astype(jnp.bfloat16)
            right = wide_r[pl.ds(h, 128, stride=16), :].astype(jnp.bfloat16)
            total = lax.dot_general(
                left, right, (((1,), (1,)), ((), ())), preferred_element_type=jnp.float32
            )
            sums.append(total.reshape(8, 8, 128))
        back[:, pl.ds(16 * pair_of, 16), :] = jnp.concatenate(sums, axis=1).astype(jnp.bfloat16)
        if pair_of % 4 == 3:
            for k in range(len(around)):
                b_part(k, pair_of // 4).start()

    def widen2(at, block):
        wide2[pl.ds(pl.multiple_of(at * 128, 128), 128), :] = block.astype(jnp.float32)

    widen2(sub * 4 + place, back[place * 2 + sub])

    for k in range(3):
        w_copy(k, other).wait_recv()
    attend_t = jnp.concatenate(
        [wa_all[s, 64 * q:64 * q + 64] for q in range(4) for s in range(2)], axis=0
    )
    bias_w = wb_all[...].reshape(32, 128)
    attout_t = turned(wo_all[...].reshape(128, 128)).astype(jnp.bfloat16)

    for k in reversed(range(len(around))):
        dg, d = around[k]
        source = peer_sub(d) * 4 + place_from(dg)
        for q in range(2):
            b_copy(k, q, 0, source).wait_recv()
        widen2(source, owned[source])

    for i in range(half):
        edgenorm = norm_rows(wide2[pl.ds(i, 128, stride=8), :]).astype(jnp.bfloat16)
        change = gates[i] * dot(outproj_t, edgenorm)
        change_t[i] = change
        first = pair_t[sub * half + i] + change
        second = norm_rows(first).astype(jnp.bfloat16)
        second_t[i] = second
        bias = dot(bias_w, second)
        for n in range(4):
            r = 16 * (n // 2) + n % 2
            bias_rows[n * 8 + i:n * 8 + i + 1, :] = bias[r:r + 1]
    bias_send[...] = bias_rows[...].astype(jnp.bfloat16)

    def c_copy(k, at):
        ds, dg, d = every[k]
        return pltpu.make_async_remote_copy(
            src_ref=bias_send, dst_ref=bias_got.at[at], send_sem=c_send.at[k], recv_sem=c_recv.at[k],
            device_id={"row": row_to(ds, dg), "sub": peer_sub(d)}, device_id_type=MESH,
        )

    scale = 1.0 / (32.0 ** 0.5)
    mine = row * 2 + sub
    for k in range(len(every)):
        c_copy(k, mine).start()
    bias_got[mine] = bias_send[...]

    for i in range(half):
        projected = dot(attend_t, second_t[i])
        query_t[i] = projected[:128].astype(jnp.bfloat16)
        keyed[i] = projected[128:256].T.astype(jnp.bfloat16)
        value_t[i] = projected[256:384].astype(jnp.bfloat16)
        attgate_t[i] = jax.nn.sigmoid(projected[384:])
    nothing = jnp.zeros((32, 128), jnp.bfloat16)
    for i in range(half):
        query = query_t[i]
        key = keyed[i]
        for n in range(4):
            head = jnp.concatenate(
                [query[32 * m:32 * m + 32] if m == n else nothing for m in range(4)], axis=0
            )
            scores_t[i, n] = dot(key, head) * scale

    for k in reversed(range(len(every))):
        ds, dg, d = every[k]
        c_copy(k, row_from(ds, dg) * 2 + peer_sub(d)).wait_recv()
    maskbias = 1000000000.0 * (mask_lanes - 1.0)
    all_bias = bias_got[...].astype(jnp.float32)
    for n in range(4):
        bias_t[n] = (all_bias[:, n * 8:n * 8 + 8, :].reshape(128, 128) + maskbias).T

    def o_copy(i, at):
        return pltpu.make_async_remote_copy(
            src_ref=out_v.at[i], dst_ref=out_ref.at[at * half + i],
            send_sem=o_send.at[i], recv_sem=o_recv.at[i],
            device_id={"sub": other}, device_id_type=MESH,
        )

    def own_copy(i):
        return pltpu.make_async_copy(out_v.at[i], out_ref.at[sub * half + i], own_sem.at[i])

    def attend_row(i):
        value = value_t[i]
        mixed = []
        for n in range(4):
            scores = scores_t[i, n] + bias_t[n]
            top = jnp.max(scores, axis=0, keepdims=True)
            weights = jnp.exp(scores - top)
            total = jnp.sum(weights, axis=0, keepdims=True)
            mixed.append(dot(value[32 * n:32 * n + 32], weights.astype(jnp.bfloat16)) / total)
        mixed = (jnp.concatenate(mixed, axis=0) * attgate_t[i]).astype(jnp.bfloat16)
        out_v[i] = (change_t[i] + dot(attout_t, mixed)).T

    for i in range(half):
        attend_row(i)
        if i % 2 == 1:
            o_copy(i - 1, sub).start()
            o_copy(i, sub).start()
            own_copy(i - 1).start()
            own_copy(i).start()

    for k in range(3):
        w_copy(k, sub).wait_send()
    for c in range(CHUNKS):
        for ds, dg in far + near:
            r_copy(ds, dg, c, place_to(dg), row).wait_send()
            if ds == 0:
                l_copy(dg, c, place_to(dg), place).wait_send()
    for k in range(len(around)):
        for q in range(2):
            b_part(k, q).wait_send()
    for k in range(len(every)):
        c_copy(k, mine).wait_send()
    for i in range(half):
        own_copy(i).wait()
        o_copy(i, sub).wait_send()
        o_copy(i, other).wait_recv()


def fused_body(pair, mask, w_edges, w_outgate, w_outproj, w_attend, w_bias, w_attout):
    f32, bf16 = jnp.float32, jnp.bfloat16
    dma = pltpu.SemaphoreType.DMA
    change = pl.pallas_call(
        fused_kernel,
        out_shape=jax.ShapeDtypeStruct(pair.shape, f32),
        in_specs=[pl.BlockSpec(memory_space=pltpu.HBM)] * 8,
        out_specs=pl.BlockSpec(memory_space=pltpu.HBM),
        scratch_shapes=[
            pltpu.VMEM((1, 128), jnp.int32),
            pltpu.VMEM((256, 128), bf16),
            pltpu.VMEM((128, 128), bf16),
            pltpu.VMEM((128, 128), bf16),
            pltpu.VMEM((256, 128), bf16),
            pltpu.VMEM((2, 128), bf16),
            pltpu.VMEM((16, 128), bf16),
            pltpu.VMEM((64, 128), bf16),
            pltpu.VMEM((8, 4, 128, 128), f32),
            pltpu.VMEM((16, 128, 128), f32),
            pltpu.VMEM((2, 256, 128), bf16),
            pltpu.VMEM((2, 16, 128), bf16),
            pltpu.VMEM((2, 64, 128), bf16),
            pltpu.VMEM((4, 16, 16, 128), bf16),
            pltpu.VMEM((4, 16, 16, 128), bf16),
            pltpu.VMEM((4, 16, 16, 128), bf16),
            pltpu.VMEM((8, 16, 16, 128), bf16),
            pltpu.VMEM((1024, 128), f32),
            pltpu.VMEM((2048, 128), f32),
            pltpu.VMEM((16, 128, 128), f32),
            pltpu.VMEM((16, 128, 128), bf16),
            pltpu.VMEM((8, 128, 128), f32),
            pltpu.VMEM((8, 128, 128), bf16),
            pltpu.VMEM((8, 128, 128), bf16),
            pltpu.VMEM((1024, 128), f32),
            pltpu.VMEM((8, 128, 128), f32),
            pltpu.VMEM((8, 128, 128), bf16),
            pltpu.VMEM((32, 128), f32),
            pltpu.VMEM((32, 128), bf16),
            pltpu.VMEM((16, 32, 128), bf16),
            pltpu.VMEM((4, 128, 128), f32),
            pltpu.VMEM((8, 128, 128), bf16),
            pltpu.VMEM((8, 128, 128), bf16),
            pltpu.VMEM((8, 128, 128), bf16),
            pltpu.VMEM((8, 128, 128), f32),
            dma((7,)),
            dma((LOADS,)),
            dma((3,)), dma((3,)),
            dma((4, CHUNKS)), dma((4, CHUNKS)),
            dma((8, CHUNKS)), dma((8, CHUNKS)),
            dma((7, 2)), dma((7, 2)),
            dma((15,)), dma((15,)),
            dma((8,)), dma((8,)), dma((8,)),
            pltpu.VMEM((8, 128, 128), f32),
        ],
        compiler_params=pltpu.CompilerParams(
            collective_id=0, has_side_effects=True, vmem_limit_bytes=60 * 1024 * 1024
        ),
        name="window",
    )(
        pair, mask.reshape(1, 128), w_edges.transpose(1, 2, 0).reshape(256, 128), w_outgate,
        w_outproj, w_attend.transpose(1, 2, 0).reshape(256, 128), w_bias.T, w_attout,
    )
    return pair + change


def fits(mesh):
    sizes = dict(mesh.shape)
    return sizes["col"] == 1 and sizes["row"] == 8 and sizes["sub"] == 2


def layer_norm(values, axis):
    mean = jnp.mean(values, axis=axis, keepdims=True)
    centred = values - mean
    variance = jnp.mean(centred * centred, axis=axis, keepdims=True)
    return centred * lax.rsqrt(variance + EPS)


def body(pair, mask, w_edges, w_outgate, w_outproj, w_attend, w_bias, w_attout):
    rows, cols, channels = pair.shape
    row_start = lax.axis_index("row") * rows
    col_start = lax.axis_index("col") * cols
    mfloat = mask.astype(jnp.float32)
    mask_rows = lax.dynamic_slice_in_dim(mfloat, row_start, rows, 0)
    mask_cols = lax.dynamic_slice_in_dim(mfloat, col_start, cols, 0)
    pmask = mask_rows[:, None] * mask_cols[None, :]
    normed = layer_norm(pair, -1).astype(jnp.bfloat16)
    projected = jnp.einsum("ijc,cqh->qhij", normed, w_edges, preferred_element_type=jnp.float32)
    left = (pmask * jax.nn.sigmoid(projected[0]) * projected[1]).astype(jnp.bfloat16)
    right = (pmask * jax.nn.sigmoid(projected[2]) * projected[3]).astype(jnp.bfloat16)
    row_count = lax.axis_size("row")
    col_count = lax.axis_size("col")
    devices = row_count * col_count
    hidden = left.shape[0]
    if devices % hidden == 0:
        groups = 1
        copies = devices // hidden
    else:
        groups = hidden // devices
        copies = 1
    share = rows // copies
    left_send = left.reshape(devices, groups * share, cols)
    right_send = jnp.repeat(right, copies, axis=0).reshape(devices, groups, rows, cols)
    left_got, right_got = (
        lax.all_to_all(left_send, ("row", "col"), split_axis=0, concat_axis=0, tiled=True),
        lax.all_to_all(right_send, ("row", "col"), split_axis=0, concat_axis=0, tiled=True),
    )
    left_owned = left_got.reshape(row_count, col_count, groups, share, cols)
    left_owned = left_owned.transpose(2, 0, 3, 1, 4).reshape(
        groups, row_count * share, col_count * cols
    )
    right_owned = right_got.reshape(row_count, col_count, groups, rows, cols)
    right_owned = right_owned.transpose(2, 0, 3, 1, 4).reshape(
        groups, row_count * rows, col_count * cols
    )
    owned_sums = jnp.einsum(
        "gak,gjk->gaj", left_owned, right_owned, preferred_element_type=jnp.float32
    )
    outgoing = owned_sums.reshape(groups, row_count, share, col_count, cols)
    outgoing = outgoing.transpose(1, 3, 0, 2, 4).reshape(devices, groups * share, cols)
    returned = lax.all_to_all(outgoing, ("row", "col"), split_axis=0, concat_axis=0, tiled=True)
    edges = returned.reshape(hidden, rows, cols)
    all_edges = lax.all_gather(edges, "sub", axis=0, tiled=True)
    edgenorm = layer_norm(all_edges, 0).astype(jnp.bfloat16)
    outgate = jax.nn.sigmoid(
        jnp.einsum("ijc,cd->ijd", normed, w_outgate, preferred_element_type=jnp.float32)
    )
    first = pair + outgate * jnp.einsum(
        "hij,hd->ijd", edgenorm, w_outproj, preferred_element_type=jnp.float32
    )
    second = layer_norm(first, -1).astype(jnp.bfloat16)
    attproj = jnp.einsum("ijc,cqe->qije", second, w_attend, preferred_element_type=jnp.float32)
    query = attproj[0].astype(jnp.bfloat16)
    keyed = attproj[1].astype(jnp.bfloat16)
    valued = attproj[2].astype(jnp.bfloat16)
    attgate = attproj[3]
    bias = jnp.einsum("ijc,ch->hij", second, w_bias, preferred_element_type=jnp.float32).astype(
        jnp.bfloat16
    )
    all_keys, all_values = (
        lax.all_gather(keyed, "col", axis=1, tiled=True),
        lax.all_gather(valued, "col", axis=1, tiled=True),
    )
    bias_full = lax.all_gather(bias, "col", axis=2, tiled=True)
    bias_every = lax.all_gather(bias_full, "row", axis=1, tiled=True)
    bias_strip = lax.dynamic_slice_in_dim(bias_every, col_start, cols, 1)
    heads = w_bias.shape[1]
    width = query.shape[2]
    head_size = width // heads
    total = all_keys.shape[1]
    query_heads = query.reshape(rows, cols, heads, head_size)
    key_heads = all_keys.reshape(rows, total, heads, head_size)
    value_heads = all_values.reshape(rows, total, heads, head_size)
    maskbias = 1000000000.0 * (mfloat - 1.0)
    scores = jnp.einsum(
        "ijhd,ikhd->hijk", query_heads, key_heads, preferred_element_type=jnp.float32
    )
    scores = scores / jnp.sqrt(jnp.float32(head_size))
    scores = scores + bias_strip.astype(jnp.float32)[:, None, :, :] + maskbias[None, None, None, :]
    weights = jax.nn.softmax(scores, axis=-1).astype(jnp.bfloat16)
    attended = jnp.einsum(
        "hijk,ikhd->ijhd", weights, value_heads, preferred_element_type=jnp.float32
    )
    mixed = (attended.reshape(rows, cols, width) * jax.nn.sigmoid(attgate)).astype(jnp.bfloat16)
    terms = jnp.einsum("ije,ec->ijc", mixed, w_attout, preferred_element_type=jnp.float32)
    summed = lax.psum(terms.astype(jnp.bfloat16), "sub").astype(jnp.float32)
    return first + summed


def solution(mesh):
    placed = (
        P(("grp", "row"), "col", None),
        P("grp"),
        P(None, None, "sub"),
        P(),
        P(),
        P(None, None, "sub"),
        P(None, "sub"),
        P("sub", None),
    )
    whole = jax.shard_map(
        body, mesh=mesh, in_specs=placed, out_specs=P(("grp", "row"), "col", None), check_vma=False
    )
    if not fits(mesh):
        return whole
    fused = jax.shard_map(
        fused_body, mesh=mesh, in_specs=placed, out_specs=P(("grp", "row"), "col", None), check_vma=False
    )
    parts = mesh.shape["grp"]
    shapes = [
        (128 * parts, 128, 128), (128 * parts,), (128, 4, 128), (128, 128), (128, 128), (128, 4, 128),
        (128, 4), (128, 128),
    ]

    def run(*arrays):
        same = [a.shape for a in arrays] == shapes
        return (fused if same else whole)(*arrays)

    return run
```
